512 devices in a mesh: stripe: 4 (over x), dp: 16 (over z_hi, y, core), tensor: 8 (over z_lo).
Axes of the slice: x: 4, y: 4, z: 16 (z_hi: 2, z_lo: 8; z = z_hi * 8 + z_lo), core: 2. Of those that a mesh axis runs over, the one named last changes fastest.
Arguments:
- normed_layer_input: bfloat16 [16384, 8192], P('dp', ('stripe', 'tensor')), may hold values from -6 to 6
- projection_output_gradient: bfloat16 [16384, 8192], P('dp', 'tensor'), may hold values from -6 to 6
- frozen_projection_weight: bfloat16 [8192, 8192], P('stripe', 'tensor'), may hold values from -0.0625 to 0.0625
- block_owner_tenant: int32 [128, 1], P('dp'), may hold values from 0 to 15
- block_token_fill: int32 [128, 1], P('dp'), may hold values from 32 to 128
- adapter_down_factors: bfloat16 [16, 48, 8192], P('dp', None, ('stripe', 'tensor')), may hold values from -0.0625 to 0.0625
- down_first_moment: float32 [16, 48, 8192], P('dp', None, ('stripe', 'tensor')), may hold values from -6 to 6
- down_second_moment: float32 [16, 48, 8192], P('dp', None, ('stripe', 'tensor')), may hold values from 1 to 100
- adapter_up_factors: bfloat16 [16, 16, 8192], P('dp', None, 'tensor'), may hold values from -0.119628906 to 0.119628906
- up_first_moment: float32 [16, 16, 8192], P('dp', None, 'tensor'), may hold values from -6 to 6
- up_second_moment: float32 [16, 16, 8192], P('dp', None, 'tensor'), may hold values from 1 to 100
Outputs:
- hidden_input_gradient: bfloat16 [16384, 8192], P('dp', ('stripe', 'tensor'))
- updated_down_factors: bfloat16 [16, 48, 8192], P('dp', None, ('stripe', 'tensor'))
- updated_down_first_moment: float32 [16, 48, 8192], P('dp', None, ('stripe', 'tensor'))
- updated_down_second_moment: float32 [16, 48, 8192], P('dp', None, ('stripe', 'tensor'))
- updated_up_factors: bfloat16 [16, 16, 8192], P('dp', None, 'tensor')
- updated_up_first_moment: float32 [16, 16, 8192], P('dp', None, 'tensor')
- updated_up_second_moment: float32 [16, 16, 8192], P('dp', None, 'tensor')
The draws below stay inside these ranges and needn't reach their ends.
All inputs are finite; a program needn't handle non-finite values.
Results may differ from the reference program's by a relative error of at most 0.019.
Values may be sent and summed in bfloat16 or wider, within the bound.
A program may use at most 64 MiB of HBM per device.

```python
import math
import jax
import jax.numpy as jnp
from jax import lax

MODEL_WIDTH = 8192
HD = 128
KVH = 8
QUERY_PER_GROUP = 6
ADAPTER_RANK = 16
BLK = 128
TOKEN_COUNT = 16384
BLOCKS = 128
TENANT_COUNT = 16
OUTPUT_COLUMNS = 8192
N_TENSOR = 8


def with_ends(array, own_key, least, high):
    extent = array.shape
    spot = [jax.random.randint(jax.random.fold_in(own_key, axis), (), 0, extent[axis]) for axis in range(len(extent))]
    array = array.at[tuple(spot)].set(least)
    longest = extent.index(max(extent))
    spot[longest] = (spot[longest] + 1) % extent[longest]
    return array.at[tuple(spot)].set(high)


def steps_of(rng, dims, cuts, smallest, high):
    gain = 1.0
    for position, shards_of in cuts:
        steps = jax.random.uniform(jax.random.fold_in(jax.random.fold_in(rng, 6), position), (shards_of,), jnp.float32, smallest / len(cuts), high / len(cuts))
        gain = gain * jnp.repeat(jnp.exp(steps), dims[position] // shards_of).reshape((-1,) + (1,) * (len(dims) - 1 - position))
    return gain


def choose_distinct(stream_key, rows, number_of, top, lift):
    sequence = jax.random.permutation(jax.random.fold_in(stream_key, 1), number_of)
    favour = sequence
    for power in range(3):
        favour = favour * favour // number_of
    favour = favour * lift // number_of
    chance = jax.random.randint(jax.random.fold_in(stream_key, 2), (rows, number_of), 0, 4096) + favour
    fixed_rows = jax.random.permutation(jax.random.fold_in(stream_key, 3), rows)[jnp.arange(number_of) % rows]
    chance = jnp.where(jnp.arange(rows)[:, None] == fixed_rows[None, :], 1 << 14, chance)
    score = chance * number_of + jnp.arange(number_of)
    return lax.top_k(score.astype(jnp.int32), top)[1].astype(jnp.int32)


def gaussian(own_key, shape, width, reach, pieces=(), kind=jnp.bfloat16):
    entries = width * jax.random.normal(own_key, shape, jnp.float32)
    if pieces:
        entries = entries * steps_of(own_key, shape, pieces, -0.22, 0.18)
    return jnp.clip(entries, -reach, reach).astype(kind)


def setup_inputs(seed: int = 0) -> dict:
    arg_keys = jax.random.split(jax.random.key(seed), 12)
    normed_layer_input = gaussian(arg_keys[0], (TOKEN_COUNT, MODEL_WIDTH), 1.0, 6.0, ((0, 16), (1, 32)))
    projection_output_gradient = gaussian(arg_keys[1], (TOKEN_COUNT, OUTPUT_COLUMNS), 1.0, 6.0, ((0, 16), (1, 8)))
    frozen_projection_weight = gaussian(arg_keys[2], (MODEL_WIDTH, OUTPUT_COLUMNS), MODEL_WIDTH ** -0.5, 0.0625, ((0, 4), (1, 8)))
    block_owner_tenant = choose_distinct(arg_keys[3], BLOCKS, TENANT_COUNT, 1, 1024)
    block_token_fill = with_ends(jax.random.randint(arg_keys[4], (BLOCKS, 1), BLK // 4, BLK + 1), jax.random.fold_in(arg_keys[4], 1), BLK // 4, BLK).astype(jnp.int32)
    adapter_down_factors = gaussian(arg_keys[5], (TENANT_COUNT, 3 * ADAPTER_RANK, MODEL_WIDTH), MODEL_WIDTH ** -0.5, 0.0625, ((0, 16), (2, 32)))
    down_first_moment = gaussian(arg_keys[6], (TENANT_COUNT, 3 * ADAPTER_RANK, MODEL_WIDTH), 1.0, 6.0, ((0, 16), (2, 32)), jnp.float32)
    down_second_moment = jnp.clip(jnp.exp(math.log(100.0) - 4.6051702 * jax.random.uniform(arg_keys[7], (TENANT_COUNT, 3 * ADAPTER_RANK, MODEL_WIDTH), jnp.float32) ** steps_of(arg_keys[7], (TENANT_COUNT, 3 * ADAPTER_RANK, MODEL_WIDTH), ((0, 16), (2, 32)), -0.2, 0.2)), 1.0, 100.0)
    adapter_up_factors = gaussian(arg_keys[8], (TENANT_COUNT, ADAPTER_RANK, OUTPUT_COLUMNS), 0.02, 0.119628906, ((0, 16), (2, 8)))
    up_first_moment = gaussian(arg_keys[9], (TENANT_COUNT, ADAPTER_RANK, OUTPUT_COLUMNS), 1.0, 6.0, ((0, 16), (2, 8)), jnp.float32)
    up_second_moment = jnp.clip(jnp.exp(math.log(100.0) - 4.6051702 * jax.random.uniform(arg_keys[10], (TENANT_COUNT, ADAPTER_RANK, OUTPUT_COLUMNS), jnp.float32) ** steps_of(arg_keys[10], (TENANT_COUNT, ADAPTER_RANK, OUTPUT_COLUMNS), ((0, 16), (2, 8)), -0.2, 0.2)), 1.0, 100.0)
    return dict(normed_layer_input=normed_layer_input, projection_output_gradient=projection_output_gradient, frozen_projection_weight=frozen_projection_weight, block_owner_tenant=block_owner_tenant, block_token_fill=block_token_fill, adapter_down_factors=adapter_down_factors, down_first_moment=down_first_moment, down_second_moment=down_second_moment, adapter_up_factors=adapter_up_factors, up_first_moment=up_first_moment, up_second_moment=up_second_moment)


adapter_scale = 2.0
beta_one = 0.9
beta_two = 0.95
adam_rate = 0.001
adam_eps = 1e-08
adam_steps = 10.0

def section_backward(grad_heads, up_factor_heads, slot_count):
    queries = jnp.einsum('btgph,brgph->btr', grad_heads[:, :, :, :slot_count], up_factor_heads[:, :, :, :slot_count], preferred_element_type=jnp.float32)
    key_part = jnp.einsum('btgh,brgh->btr', grad_heads[:, :, :, slot_count], up_factor_heads[:, :, :, slot_count], preferred_element_type=jnp.float32)
    value_part = jnp.einsum('btgh,brgh->btr', grad_heads[:, :, :, slot_count + 1], up_factor_heads[:, :, :, slot_count + 1], preferred_element_type=jnp.float32)
    return jnp.concatenate([queries, key_part, value_part], axis=2)

def section_gradient(low_heads, grad_heads, slot_count):
    rank_size = low_heads.shape[2] // 3
    queries = jnp.einsum('btr,btgph->brgph', low_heads[:, :, :rank_size], grad_heads[:, :, :, :slot_count], preferred_element_type=jnp.float32)
    key_part = jnp.einsum('btr,btgh->brgh', low_heads[:, :, rank_size:2 * rank_size], grad_heads[:, :, :, slot_count], preferred_element_type=jnp.float32)
    value_part = jnp.einsum('btr,btgh->brgh', low_heads[:, :, 2 * rank_size:], grad_heads[:, :, :, slot_count + 1], preferred_element_type=jnp.float32)
    joined = jnp.concatenate([queries, key_part[:, :, :, None], value_part[:, :, :, None]], axis=3)
    return joined.reshape(joined.shape[0], joined.shape[1], -1)

def apply_adam_update(params, moment, second, gradient):
    moment_new = beta_one * moment + (1.0 - beta_one) * gradient
    second_new = beta_two * second + (1.0 - beta_two) * (gradient * gradient)
    first_fix = moment_new / (1.0 - beta_one ** adam_steps)
    second_fix = second_new / (1.0 - beta_two ** adam_steps)
    stepped = params.astype(jnp.float32) - adam_rate * first_fix / (jnp.sqrt(second_fix) + adam_eps)
    return (stepped.astype(jnp.bfloat16), moment_new, second_new)

def reference(normed_layer_input, projection_output_gradient, frozen_projection_weight, block_owner_tenant, block_token_fill, adapter_down_factors, down_first_moment, down_second_moment, adapter_up_factors, up_first_moment, up_second_moment):
    tenant_index = block_owner_tenant[:, 0]
    places = jnp.arange(BLK, dtype=jnp.int32)
    usable = places[None, :] < block_token_fill[:, 0][:, None]
    grad_blocks = projection_output_gradient.reshape(BLOCKS, BLK, OUTPUT_COLUMNS)
    masked = jnp.where(usable[:, :, None], grad_blocks, jnp.zeros_like(grad_blocks))
    hid_blocks = normed_layer_input.reshape(BLOCKS, BLK, MODEL_WIDTH).astype(jnp.float32)
    down_chosen_factor = adapter_down_factors[tenant_index].astype(jnp.float32)
    up_chosen_factor = adapter_up_factors[tenant_index].astype(jnp.float32)
    head_mask_rows = masked.astype(jnp.float32).reshape(BLOCKS, BLK, KVH, QUERY_PER_GROUP + 2, HD)
    up_factor_heads = up_chosen_factor.reshape(BLOCKS, ADAPTER_RANK, KVH, QUERY_PER_GROUP + 2, HD)
    lowrank_full = jnp.einsum('btd,brd->btr', hid_blocks, down_chosen_factor)
    backward_full = adapter_scale * section_backward(head_mask_rows, up_factor_heads, QUERY_PER_GROUP)
    masked_flat = masked.reshape(TOKEN_COUNT, OUTPUT_COLUMNS)
    part_cols = OUTPUT_COLUMNS // N_TENSOR
    frozen_total = jnp.zeros((TOKEN_COUNT, MODEL_WIDTH), jnp.float32)
    for shard in range(N_TENSOR):
        first = shard * part_cols
        partial_prod = jnp.dot(masked_flat[:, first:first + part_cols], frozen_projection_weight[:, first:first + part_cols].T, preferred_element_type=jnp.float32)
        rounded = lax.optimization_barrier(partial_prod.astype(jnp.bfloat16))
        frozen_total = frozen_total + rounded.astype(jnp.float32)
    adapter_input = jnp.einsum('lpm,lmw->lpw', backward_full, down_chosen_factor)
    hidden_input_gradient = (frozen_total + adapter_input.reshape(TOKEN_COUNT, MODEL_WIDTH)).astype(jnp.bfloat16)
    down_block = jnp.einsum('btr,btd->brd', backward_full, hid_blocks)
    up_factor_block = adapter_scale * section_gradient(lowrank_full, head_mask_rows, QUERY_PER_GROUP)
    owners = (tenant_index[:, None] == jnp.arange(TENANT_COUNT, dtype=jnp.int32)[None, :]).astype(jnp.float32)
    down_factor_gradient = jnp.einsum('bn,brd->nrd', owners, down_block, precision=lax.Precision.HIGHEST)
    up_factor_gradient = jnp.einsum('bn,brc->nrc', owners, up_factor_block, precision=lax.Precision.HIGHEST)
    updated_down_factors, updated_down_first_moment, updated_down_second_moment = apply_adam_update(adapter_down_factors, down_first_moment, down_second_moment, down_factor_gradient)
    updated_up_factors, updated_up_first_moment, updated_up_second_moment = apply_adam_update(adapter_up_factors, up_first_moment, up_second_moment, up_factor_gradient)
    return (hidden_input_gradient, updated_down_factors, updated_down_first_moment, updated_down_second_moment, updated_up_factors, updated_up_first_moment, updated_up_second_moment)
```

```python
import functools

import jax
import jax.numpy as jnp
from jax import lax
from jax.experimental import pallas as pl
from jax.experimental.pallas import tpu as pltpu
from jax.sharding import PartitionSpec as P

BLK = 128
RANK = 16
DOWN = 48
FAC = 64
PIECES = 4
SKEW = 2
AHEAD = 2

adapter_scale = 2.0
beta_one = 0.9
beta_two = 0.95
adam_rate = 0.001
adam_eps = 1e-08
adam_steps = 10.0

F32 = jnp.float32
BF16 = jnp.bfloat16
MESH = pl.DeviceIdType.MESH

AT_FORWARD = 1
AT_PROJECT = 3
AT_STRIPE_SUM = 5
AT_TENSOR_SUM = 6
AT_STRIPE_SPREAD = 8
AT_GRADIENT = 9
AT_GROUP_SUM = 12
AT_HALF_SUM = 15
AT_UP_ADAM = 17


def adam(params, moment, second, gradient):
    moment_new = beta_one * moment + (1.0 - beta_one) * gradient
    second_new = beta_two * second + (1.0 - beta_two) * (gradient * gradient)
    first_fix = moment_new / (1.0 - beta_one**adam_steps)
    second_fix = second_new / (1.0 - beta_two**adam_steps)
    stepped = params.astype(F32) - adam_rate * first_fix / (jnp.sqrt(second_fix) + adam_eps)
    return stepped.astype(BF16), moment_new, second_new


def kernel(
    S, NP, NT,
    ten_ref, fill_ref,
    x_in, a_in, w_in, dn_in, dm_in, dv_in, up_in, um_in, uv_in,
    out_o, dn_o, dm_o, dv_o, up_o, um_o, uv_o,
    av, wv, xv, fac, pv, rv,
    lp, xrs, xs, zrs, lb,
    gl, ul, gp, grs, go, gs, gz, ux, acc, ov,
    dmv, dvv, umv, uvv, upv, dnn, upn,
    load_sem, w_sem, out_sem, store_sem,
    line_send, line_recv,
    fac_send, fac_recv,
    xr_send, xr_recv, zr_send, zr_recv, za_send, za_recv, xa_send, xa_recv,
    gr_send, gr_recv, gz_send, gz_recv, ux_send, ux_recv,
):
    G = NP // 2
    TOK, C = av.shape
    D = xv.shape[1]
    NB = TOK // BLK
    QT = TOK // S
    CQ = C // S
    HALF = CQ // 2
    PR = TOK // PIECES
    CHUNK = wv.shape[0] // NT
    s = lax.axis_index("stripe")
    p = lax.axis_index("dp")
    t = lax.axis_index("tensor")
    zh = lax.div(p, G)
    m = lax.rem(p, G)
    pz = (1 - zh) * G + m

    def other(axis, here, size, o):
        return {axis: lax.rem(here + o, size)}

    def group_peer(o):
        return zh * G + lax.rem(m + o, G)

    quarter = pl.ds(pl.multiple_of(s * CQ, CQ), CQ)
    my_tokens = pl.ds(pl.multiple_of(s * QT, QT), QT)
    loads = [
        pltpu.make_async_copy(dn_in.at[0], fac.at[p, pl.ds(0, DOWN)], load_sem.at[0]),
        pltpu.make_async_copy(up_in.at[0, :, quarter], fac.at[p, pl.ds(DOWN, RANK)], load_sem.at[1]),
        pltpu.make_async_copy(a_in, av, load_sem.at[2]),
        pltpu.make_async_copy(x_in, xv, load_sem.at[3]),
        pltpu.make_async_copy(dm_in.at[0], dmv, load_sem.at[4]),
        pltpu.make_async_copy(dv_in.at[0], dvv, load_sem.at[5]),
        pltpu.make_async_copy(um_in.at[0], umv, load_sem.at[6]),
        pltpu.make_async_copy(uv_in.at[0], uvv, load_sem.at[7]),
        pltpu.make_async_copy(up_in.at[0], upv, load_sem.at[8]),
    ]

    def order(i):
        inner = jnp.where(lax.rem(i, 2) == 0, NT - 1 - lax.div(i, 2), lax.div(i, 2))
        return jnp.where(t == 0, NT - 1 - i, jnp.where(t == NT - 1, i, inner))

    def w_load(j):
        rows = pl.ds(pl.multiple_of(j * CHUNK, CHUNK), CHUNK)
        return pltpu.make_async_copy(w_in.at[rows], wv.at[rows], w_sem.at[j])

    for load in loads[:3]:
        load.start()
    for i in range(NT):
        w_load(order(jnp.int32(i))).start()
    for load in loads[3:]:
        load.start()

    barrier = pltpu.get_barrier_semaphore()
    partners = [other("tensor", t, NT, o) for o in range(1, NT)]
    partners += [other("stripe", s, S, o) for o in range(1, S)]
    partners += [{"dp": group_peer(o)} for o in range(1, G)]
    partners += [{"dp": pz}]
    for partner in partners:
        pl.semaphore_signal(barrier, inc=1, device_id=partner, device_id_type=MESH)

    loads[2].wait()

    @pl.loop(0, NB)
    def _(b):
        rows = pl.ds(pl.multiple_of(b * BLK, BLK), BLK)
        place = lax.broadcasted_iota(jnp.int32, (BLK, C), 0)
        block = av[rows, :]
        av[rows, :] = jnp.where(place < fill_ref[b, 0], block, jnp.zeros_like(block))

    loads[0].wait()
    loads[1].wait()
    pl.semaphore_wait(barrier, len(partners))

    def remote(src, dst, send, recv, device):
        return pltpu.make_async_remote_copy(
            src_ref=src, dst_ref=dst, send_sem=send, recv_sem=recv, device_id=device, device_id_type=MESH
        )

    def fac_copy(slot, i, device):
        return remote(fac.at[slot], fac.at[slot], fac_send.at[i], fac_recv.at[slot], device)

    def xr_copy(o):
        to = lax.rem(s + o, S)
        lanes = pl.ds(pl.multiple_of(to * QT, QT), QT)
        return remote(lp.at[:, lanes], xrs.at[s], xr_send.at[o], xr_recv.at[s], {"stripe": to})

    def owner(g):
        return (g + 1) % NT

    def section(g):
        return pl.ds(g * RANK, RANK)

    def zr_copy(g):
        return remote(xs.at[section(g)], zrs.at[g, t], zr_send.at[g], zr_recv.at[g, t], {"tensor": owner(g)})

    def za_copy(g, o):
        part = lb.at[section(g), my_tokens]
        return remote(part, part, za_send.at[g, o], za_recv.at[g], other("tensor", t, NT, o))

    def xa_copy(o):
        part = lb.at[:, my_tokens]
        return remote(part, part, xa_send.at[o], xa_recv.at[s], other("stripe", s, S, o))

    def gr_copy(o):
        to = lax.rem(m + o, G)
        return remote(gp.at[to], grs.at[m], gr_send.at[o], gr_recv.at[m], {"dp": zh * G + to})

    def gz_copy():
        return remote(gs, gz, gz_send, gz_recv, {"dp": pz})

    def ux_copy(o):
        return remote(ux.at[s], ux.at[s], ux_send.at[o], ux_recv.at[s], other("stripe", s, S, o))

    fac_copy(p, 0, {"dp": pz}).start()
    for o in range(1, G):
        fac_copy(p, o, {"dp": group_peer(o)}).start()

    def forward():
        fac_copy(pz, 0, {"dp": pz}).wait_recv()
        for o in range(1, G):
            fac_copy(pz, G + o, {"dp": group_peer(o)}).start()

    def project():
        for o in range(1, G):
            fac_copy(zh * G + lax.rem(m + o, G), 0, {"dp": pz}).wait_recv()
            fac_copy((1 - zh) * G + lax.rem(m + o, G), 0, {"dp": pz}).wait_recv()
        loads[3].wait()
        last = s == S - 1
        zero = jnp.zeros((RANK, BLK), F32)

        @pl.loop(0, NB)
        def _(b):
            rows = pl.ds(pl.multiple_of(b * BLK, BLK), BLK)
            chosen = fac[ten_ref[b, 0]]
            nt = (((1,), (1,)), ((), ()))
            low = lax.dot_general(chosen[:DOWN], xv[rows, :], nt, preferred_element_type=F32)
            grad = av[rows, quarter]
            first = lax.dot_general(chosen[DOWN:, :HALF], grad[:, :HALF], nt, preferred_element_type=F32)
            second = lax.dot_general(chosen[DOWN:, HALF:], grad[:, HALF:], nt, preferred_element_type=F32)
            both = jnp.concatenate(
                [
                    low,
                    jnp.where(last, zero, first + second),
                    jnp.where(last, first, zero),
                    jnp.where(last, second, zero),
                ],
                axis=0,
            )
            lp[:, rows] = (adapter_scale * both).astype(BF16)

        for o in range(1, S):
            xr_copy(o).start()

    def stripe_sum():
        total = lp[:, my_tokens].astype(F32)
        for o in range(1, S):
            src = lax.rem(s + o, S)
            remote(xs, xrs.at[src], xr_send.at[0], xr_recv.at[src], {"dp": pz}).wait_recv()
            total += xrs[src].astype(F32)
        xs[...] = total.astype(BF16)
        for g in range(6):

            @pl.when(t != owner(g))
            def _(g=g):
                zr_copy(g).start()

    def tensor_sum():
        for g in range(6):

            @pl.when(t == owner(g))
            def _(g=g):
                def add(o, total):
                    src = lax.rem(t + o, NT)
                    remote(
                        xs.at[section(g)], zrs.at[g, src], zr_send.at[g], zr_recv.at[g, src], {"dp": pz}
                    ).wait_recv()
                    return total + zrs[g, src].astype(F32)

                total = lax.fori_loop(1, NT, add, xs[section(g), :].astype(F32))
                lb[section(g), my_tokens] = total.astype(BF16)
                for o in range(1, NT):
                    za_copy(g, o).start()

    def stripe_spread():
        for g in range(6):

            @pl.when(t != owner(g))
            def _(g=g):
                za_copy(g, 1).wait_recv()

        for o in range(1, S):
            xa_copy(o).start()

    group = min(4, NP)

    def gradient():
        for o in range(1, S):
            src = lax.rem(s + o, S)
            part = lb.at[:, pl.ds(pl.multiple_of(src * QT, QT), QT)]
            remote(part, part, xa_send.at[0], xa_recv.at[src], {"dp": pz}).wait_recv()
        block_of = lax.div(lax.broadcasted_iota(jnp.int32, (1, TOK), 1), BLK)
        tenant = jnp.zeros((1, TOK), jnp.int32)
        for b in range(NB):
            tenant = jnp.where(block_of == b, ten_ref[b, 0], tenant)
        last = s == S - 1
        sec_first = jnp.where(last, RANK, 0)
        sec_second = jnp.where(last, 2 * RANK, 0)

        @pl.loop(0, NP)
        def _(n):
            here = jnp.where(tenant == n, 1.0, 0.0).astype(BF16)
            gl[pl.ds(pl.multiple_of(n * DOWN, RANK), DOWN), :] = lb[pl.ds(DOWN, DOWN), :] * here
            rows = pl.ds(pl.multiple_of(n * RANK, RANK), RANK)
            ul[0, rows, :] = lb[pl.ds(pl.multiple_of(sec_first, RANK), RANK), :] * here
            ul[1, rows, :] = lb[pl.ds(pl.multiple_of(sec_second, RANK), RANK), :] * here

        @pl.loop(0, NP // group)
        def _(i):
            rows = pl.ds(pl.multiple_of(i * group * DOWN, RANK), group * DOWN)
            part = jnp.dot(gl[rows, :], xv[...], preferred_element_type=F32).astype(BF16)
            for e in range(group):
                n = i * group + e
                gp[lax.rem(n, G), lax.div(n, G), :DOWN, :] = part[e * DOWN : (e + 1) * DOWN]

        for h in range(2):
            lanes = pl.ds(pl.multiple_of(s * CQ + h * HALF, HALF), HALF)
            part = jnp.dot(ul[h], av[:, lanes], preferred_element_type=F32).astype(BF16)
            for n in range(NP):
                gp[n % G, n // G, DOWN:, h * HALF : (h + 1) * HALF] = part[n * RANK : (n + 1) * RANK]

        for o in range(1, G):
            gr_copy(o).start()

        @pl.loop(0, NB)
        def _(b):
            rows = pl.ds(pl.multiple_of(b * BLK, BLK), BLK)
            down = fac[ten_ref[b, 0]][:DOWN]
            extra = lax.dot_general(
                lb[pl.ds(DOWN, DOWN), rows], down, (((0,), (0,)), ((), ())), preferred_element_type=F32
            )
            acc[rows, :] = extra + pv[t, rows, :].astype(F32)

    def group_sum():
        for o in range(1, G):
            src = lax.rem(m + o, G)
            remote(gp.at[0], grs.at[src], gr_send.at[0], gr_recv.at[src], {"dp": pz}).wait_recv()

        def total(half):
            value = gp[m, half].astype(F32)
            for o in range(1, G):
                value += grs[lax.rem(m + o, G), half].astype(F32)
            return value

        gs[...] = total(1 - zh).astype(BF16)
        gz_copy().start()
        go[...] = total(zh)

    def half_sum():
        gz_copy().wait_recv()
        grad = go[...] + gz[...].astype(F32)
        ux[s] = grad[DOWN:]
        for o in range(1, S):
            ux_copy(o).start()
        for load in loads[4:]:
            load.wait()
        dnn[...], dmv[...], dvv[...] = adam(fac[p, :DOWN, :], dmv[...], dvv[...], grad[:DOWN])
        for store in stores[:3]:
            store.start()

    def up_adam():
        for o in range(1, S):
            src = lax.rem(s + o, S)
            remote(ux.at[src], ux.at[src], ux_send.at[0], ux_recv.at[src], {"dp": pz}).wait_recv()
        for i in range(S):
            lanes = pl.ds(i * CQ, CQ)
            upn[:, lanes], umv[:, lanes], uvv[:, lanes] = adam(
                upv[:, lanes], umv[:, lanes], uvv[:, lanes], ux[i]
            )
        for store in stores[3:]:
            store.start()

    stores = [
        pltpu.make_async_copy(dnn, dn_o.at[0], store_sem.at[0]),
        pltpu.make_async_copy(dmv, dm_o.at[0], store_sem.at[1]),
        pltpu.make_async_copy(dvv, dv_o.at[0], store_sem.at[2]),
        pltpu.make_async_copy(upn, up_o.at[0], store_sem.at[3]),
        pltpu.make_async_copy(umv, um_o.at[0], store_sem.at[4]),
        pltpu.make_async_copy(uvv, uv_o.at[0], store_sem.at[5]),
    ]

    def multiply(i):
        j = order(i)
        w_load(j).wait()

        @pl.loop(0, PIECES)
        def _(q):
            rows = pl.ds(pl.multiple_of(q * PR, PR), PR)
            part = lax.dot_general(
                av[rows, :],
                wv[pl.ds(pl.multiple_of(j * CHUNK, CHUNK), CHUNK), :],
                (((1,), (1,)), ((), ())),
                preferred_element_type=F32,
            )
            pv[j, rows, :] = part.astype(BF16)

    def rank(way):
        return t if way == 0 else NT - 1 - t

    def line_copy(way, u):
        k, q = lax.div(u, PIECES), lax.rem(u, PIECES)
        j = NT - 1 - k if way == 0 else k
        rows = pl.ds(pl.multiple_of(q * PR, PR), PR)
        to = t + 1 if way == 0 else t - 1
        return j, rows, remote(
            pv.at[j, rows], rv.at[way, j, rows], line_send.at[j, q], line_recv.at[way, j, q], {"tensor": to}
        )

    def line_step(v):
        for way in range(2):
            r = rank(way)
            u = v - SKEW * r

            @pl.when((u >= 0) & (u < (NT - 1 - r) * PIECES))
            def _(way=way, r=r, u=u):
                j, rows, copy = line_copy(way, u)

                @pl.when(r > 0)
                def _():
                    copy.wait_recv()
                    pv[j, rows, :] = (pv[j, rows, :].astype(F32) + rv[way, j, rows, :].astype(F32)).astype(BF16)

                @pl.when(u >= AHEAD)
                def _():
                    line_copy(way, u - AHEAD)[2].wait_send()

                copy.start()

    stages = [
        (AT_FORWARD, forward),
        (AT_PROJECT, project),
        (AT_STRIPE_SUM, stripe_sum),
        (AT_TENSOR_SUM, tensor_sum),
        (AT_STRIPE_SPREAD, stripe_spread),
        (AT_GRADIENT, gradient),
        (AT_GROUP_SUM, group_sum),
        (AT_HALF_SUM, half_sum),
        (AT_UP_ADAM, up_adam),
    ]
    steps = max((NT - 1 - r) * PIECES + SKEW * r for r in range(NT - 1))
    steps = max(steps, AT_UP_ADAM + 1, NT)

    @pl.loop(0, steps)
    def _(v):
        @pl.when(v < NT)
        def _():
            multiply(v)

        line_step(v)
        for at, stage in stages:
            pl.when(v == at)(stage)

    def finish(q):
        rows = pl.ds(q * PR, PR)
        for way in range(2):

            @pl.when(rank(way) > 0)
            def _(way=way):
                part = rv.at[way, t, rows]
                remote(part, part, line_send.at[t, q], line_recv.at[way, t, q], {"dp": pz}).wait_recv()
                acc[rows, :] += rv[way, t, rows, :].astype(F32)

        ov[rows, :] = acc[rows, :].astype(BF16)
        return pltpu.make_async_copy(ov.at[rows], out_o.at[rows], out_sem.at[q])

    writes = []
    for q in range(PIECES):
        write = finish(q)
        write.start()
        writes.append(write)

    for way in range(2):
        r = rank(way)

        @pl.when(r < NT - 1)
        def _(way=way, r=r):
            for back in range(AHEAD):
                line_copy(way, (NT - 1 - r) * PIECES - AHEAD + back)[2].wait_send()

    fac_copy(p, 0, {"dp": pz}).wait_send()
    for o in range(1, G):
        fac_copy(p, o, {"dp": group_peer(o)}).wait_send()
        fac_copy(pz, G + o, {"dp": group_peer(o)}).wait_send()
        gr_copy(o).wait_send()
    for o in range(1, S):
        xr_copy(o).wait_send()
        xa_copy(o).wait_send()
        ux_copy(o).wait_send()
    for g in range(6):

        @pl.when(t != owner(g))
        def _(g=g):
            zr_copy(g).wait_send()

        @pl.when(t == owner(g))
        def _(g=g):
            for o in range(1, NT):
                za_copy(g, o).wait_send()

    gz_copy().wait_send()
    for store in stores:
        store.wait()
    for write in writes:
        write.wait()


def on_device(
    S, NP, NT,
    normed_layer_input,
    projection_output_gradient,
    frozen_projection_weight,
    block_owner_tenant,
    block_token_fill,
    adapter_down_factors,
    down_first_moment,
    down_second_moment,
    adapter_up_factors,
    up_first_moment,
    up_second_moment,
):
    tok, d = normed_layer_input.shape
    c = projection_output_gradient.shape[1]
    w_rows = frozen_projection_weight.shape[0]
    G = NP // 2
    qt = tok // S
    any_space = pl.BlockSpec(memory_space=pl.ANY)
    smem = pl.BlockSpec(memory_space=pltpu.SMEM)
    outs = (
        jax.ShapeDtypeStruct((tok, d), BF16),
        jax.ShapeDtypeStruct(adapter_down_factors.shape, BF16),
        jax.ShapeDtypeStruct(down_first_moment.shape, F32),
        jax.ShapeDtypeStruct(down_second_moment.shape, F32),
        jax.ShapeDtypeStruct(adapter_up_factors.shape, BF16),
        jax.ShapeDtypeStruct(up_first_moment.shape, F32),
        jax.ShapeDtypeStruct(up_second_moment.shape, F32),
    )
    vm, dma = pltpu.VMEM, pltpu.SemaphoreType.DMA
    scratch = [
        vm((tok, c), BF16),
        vm((w_rows, c), BF16),
        vm((tok, d), BF16),
        vm((NP, FAC, d), BF16),
        vm((NT, tok, w_rows // NT), BF16),
        vm((2, NT, tok, w_rows // NT), BF16),
        vm((2 * DOWN, tok), BF16),
        vm((S, 2 * DOWN, qt), BF16),
        vm((2 * DOWN, qt), BF16),
        vm((6, NT, RANK, qt), BF16),
        vm((2 * DOWN, tok), BF16),
        vm((NP * DOWN, tok), BF16),
        vm((2, NP * RANK, tok), BF16),
        vm((G, 2, FAC, d), BF16),
        vm((G, 2, FAC, d), BF16),
        vm((FAC, d), F32),
        vm((FAC, d), BF16),
        vm((FAC, d), BF16),
        vm((S, RANK, c // S), F32),
        vm((tok, d), F32),
        vm((tok, d), BF16),
        vm((DOWN, d), F32),
        vm((DOWN, d), F32),
        vm((RANK, c), F32),
        vm((RANK, c), F32),
        vm((RANK, c), BF16),
        vm((DOWN, d), BF16),
        vm((RANK, c), BF16),
        dma((9,)), dma((NT,)), dma((PIECES,)), dma((6,)),
        dma((NT, PIECES)), dma((2, NT, PIECES)),
        dma((2 * G,)), dma((NP,)),
        dma((S,)), dma((S,)), dma((6,)), dma((6, NT)), dma((6, NT)), dma((6,)), dma((S,)), dma((S,)),
        dma((G,)), dma((G,)), dma, dma, dma((S,)), dma((S,)),
    ]
    return pl.pallas_call(
        functools.partial(kernel, S, NP, NT),
        out_shape=outs,
        in_specs=[smem] * 2 + [any_space] * 9,
        out_specs=[any_space] * 7,
        scratch_shapes=scratch,
        compiler_params=pltpu.CompilerParams(
            collective_id=0, has_side_effects=True, vmem_limit_bytes=48 * 1024 * 1024
        ),
        cost_estimate=pl.CostEstimate(
            flops=2 * tok * c * w_rows, bytes_accessed=2 * (tok * c + w_rows * c), transcendentals=0
        ),
        name="united_backward",
    )(
        block_owner_tenant,
        block_token_fill,
        normed_layer_input,
        projection_output_gradient,
        frozen_projection_weight,
        adapter_down_factors,
        down_first_moment,
        down_second_moment,
        adapter_up_factors,
        up_first_moment,
        up_second_moment,
    )


def solution(mesh):
    both = ("stripe", "tensor")
    return jax.shard_map(
        functools.partial(on_device, mesh.shape["stripe"], mesh.shape["dp"], mesh.shape["tensor"]),
        mesh=mesh,
        in_specs=(
            P("dp", both),
            P("dp", "tensor"),
            P("stripe", "tensor"),
            P("dp", None),
            P("dp", None),
            P("dp", None, both),
            P("dp", None, both),
            P("dp", None, both),
            P("dp", None, "tensor"),
            P("dp", None, "tensor"),
            P("dp", None, "tensor"),
        ),
        out_specs=(
            P("dp", both),
            P("dp", None, both),
            P("dp", None, both),
            P("dp", None, both),
            P("dp", None, "tensor"),
            P("dp", None, "tensor"),
            P("dp", None, "tensor"),
        ),
        check_vma=False,
    )
```

```python
import functools

import jax
import jax.numpy as jnp
from jax import lax
from jax.experimental import pallas as pl
from jax.experimental.pallas import tpu as pltpu
from jax.sharding import PartitionSpec as P

BLK = 128
RANK = 16
DOWN = 48
FAC = 64
PIECES = 4
SKEW = 2
AHEAD = 4
VMEM_BYTES = 62 * 1024 * 1024

adapter_scale = 2.0
beta_one = 0.9
beta_two = 0.95
adam_rate = 0.001
adam_eps = 1e-08
adam_steps = 10.0

F32 = jnp.float32
BF16 = jnp.bfloat16
MESH = pl.DeviceIdType.MESH

AT_GREET = 0
AT_EXCHANGE = 4
AT_FORWARD = 7
AT_PROJECT = 9
AT_STRIPE_SUM = 11
AT_TENSOR_SUM = 13
AT_STRIPE_SPREAD = 15
AT_GRADIENT = 17
AT_ADAPTER = 19
AT_GROUP_SUM = 21
AT_HALF_SUM = 24
AT_UP_ADAM = 26


def adam(params, moment, second, gradient):
    moment_new = beta_one * moment + (1.0 - beta_one) * gradient
    second_new = beta_two * second + (1.0 - beta_two) * (gradient * gradient)
    first_fix = moment_new / (1.0 - beta_one**adam_steps)
    second_fix = second_new / (1.0 - beta_two**adam_steps)
    stepped = params.astype(F32) - adam_rate * first_fix / (jnp.sqrt(second_fix) + adam_eps)
    return stepped.astype(BF16), moment_new, second_new


def kernel(
    S, NP, NT,
    ten_ref, fill_ref,
    x_in, a_in, w_in, dn_in, dm_in, dv_in, up_in, um_in, uv_in,
    out_o, dn_o, dm_o, dv_o, up_o, um_o, uv_o,
    av, wv, xv, fac, pv, rv,
    lp, xrs, xs, zrs, lb,
    gl, ul, gp, grs, go, gs, gz, ux, acc, ov,
    dmv, dvv, umv, uvv, upv, dnn, upn,
    load_sem, w_sem, out_sem, store_sem,
    line_send, line_recv,
    fac_send, fac_recv,
    xr_send, xr_recv, zr_send, zr_recv, za_send, za_recv, xa_send, xa_recv,
    gr_send, gr_recv, gz_send, gz_recv, ux_send, ux_recv, hello,
):
    G = NP // 2
    TOK, C = av.shape
    D = xv.shape[1]
    NB = TOK // BLK
    QT = TOK // S
    CQ = C // S
    HALF = CQ // 2
    PR = TOK // PIECES
    CHUNK = wv.shape[0] // NT
    s = lax.axis_index("stripe")
    p = lax.axis_index("dp")
    t = lax.axis_index("tensor")
    zh = lax.div(p, G)
    m = lax.rem(p, G)
    pz = (1 - zh) * G + m

    def other(axis, here, size, o):
        return {axis: lax.rem(here + o, size)}

    def group_peer(o):
        return zh * G + lax.rem(m + o, G)

    quarter = pl.ds(pl.multiple_of(s * CQ, CQ), CQ)
    my_tokens = pl.ds(pl.multiple_of(s * QT, QT), QT)
    loads = [
        pltpu.make_async_copy(dn_in.at[0], fac.at[p, pl.ds(0, DOWN)], load_sem.at[0]),
        pltpu.make_async_copy(up_in.at[0, :, quarter], fac.at[p, pl.ds(DOWN, RANK)], load_sem.at[1]),
        pltpu.make_async_copy(a_in, av, load_sem.at[2]),
        pltpu.make_async_copy(x_in, xv, load_sem.at[3]),
        pltpu.make_async_copy(dm_in.at[0], dmv, load_sem.at[4]),
        pltpu.make_async_copy(dv_in.at[0], dvv, load_sem.at[5]),
        pltpu.make_async_copy(um_in.at[0], umv, load_sem.at[6]),
        pltpu.make_async_copy(uv_in.at[0], uvv, load_sem.at[7]),
        pltpu.make_async_copy(up_in.at[0], upv, load_sem.at[8]),
    ]

    def order(i):
        inner = jnp.where(lax.rem(i, 2) == 0, NT - 1 - lax.div(i, 2), lax.div(i, 2))
        return jnp.where(t == 0, NT - 1 - i, jnp.where(t == NT - 1, i, inner))

    def w_load(j):
        rows = pl.ds(pl.multiple_of(j * CHUNK, CHUNK), CHUNK)
        return pltpu.make_async_copy(w_in.at[rows], wv.at[rows], w_sem.at[j])

    for load in loads[:3]:
        load.start()
    for i in range(NT):
        w_load(order(jnp.int32(i))).start()
    for load in loads[3:]:
        load.start()

    z = zh * NT + t
    after = {"dp": jnp.where(t == NT - 1, p + G, p), "tensor": lax.rem(t + 1, NT)}
    before = {"dp": jnp.where(t == 0, p - G, p), "tensor": lax.rem(t + NT - 1, NT)}
    has_after, has_before = z < 2 * NT - 1, z > 0
    barrier = pltpu.get_barrier_semaphore()
    partners = [other("stripe", s, S, o) for o in range(1, S)]
    partners += [{"dp": group_peer(o)} for o in range(1, G)]
    for partner in partners:
        pl.semaphore_signal(barrier, inc=1, device_id=partner, device_id_type=MESH)
    for there, partner in ((has_after, after), (has_before, before)):

        @pl.when(there)
        def _(partner=partner):
            pl.semaphore_signal(barrier, inc=1, device_id=partner, device_id_type=MESH)

    loads[2].wait()

    @pl.loop(0, NB)
    def _(b):
        rows = pl.ds(pl.multiple_of(b * BLK, BLK), BLK)
        place = lax.broadcasted_iota(jnp.int32, (BLK, C), 0)
        block = av[rows, :]
        av[rows, :] = jnp.where(place < fill_ref[0, b], block, jnp.zeros_like(block))

    def multiply(i):
        j = order(i)
        w_load(j).wait()
        part = lax.dot_general(
            av[...],
            wv[pl.ds(pl.multiple_of(j * CHUNK, CHUNK), CHUNK), :],
            (((1,), (1,)), ((), ())),
            preferred_element_type=F32,
        )
        pv[j] = part.astype(BF16)

    multiply(jnp.int32(0))

    loads[0].wait()
    loads[1].wait()
    pl.semaphore_wait(barrier, len(partners) + jnp.where(has_after & has_before, 2, 1))

    def greet(slot):
        for way, to, there in ((0, after, has_after), (1, before, has_before)):
            r = z if way == 0 else 2 * NT - 1 - z
            if slot >= 1:

                @pl.when(r >= slot + 1)
                def _(way=way):
                    pl.semaphore_wait(hello.at[way, slot], 1)

            if slot + 1 < NT:

                @pl.when((r >= slot + 1) & there)
                def _(way=way, to=to):
                    pl.semaphore_signal(hello.at[way, slot + 1], inc=1, device_id=to, device_id_type=MESH)

    greet(0)

    def remote(src, dst, send, recv, device):
        return pltpu.make_async_remote_copy(
            src_ref=src, dst_ref=dst, send_sem=send, recv_sem=recv, device_id=device, device_id_type=MESH
        )

    def fac_copy(slot, i, device):
        return remote(fac.at[slot], fac.at[slot], fac_send.at[i], fac_recv.at[slot], device)

    def xr_copy(o):
        to = lax.rem(s + o, S)
        lanes = pl.ds(pl.multiple_of(to * QT, QT), QT)
        return remote(lp.at[:, lanes], xrs.at[s], xr_send.at[o], xr_recv.at[s], {"stripe": to})

    def owner(g):
        return (g + 1) % NT

    def section(g):
        return pl.ds(g * RANK, RANK)

    def zr_copy(g):
        return remote(xs.at[section(g)], zrs.at[g, t], zr_send.at[g], zr_recv.at[g, t], {"tensor": owner(g)})

    def za_copy(g, o):
        part = lb.at[section(g), my_tokens]
        return remote(part, part, za_send.at[g, o], za_recv.at[g], other("tensor", t, NT, o))

    def xa_copy(o):
        part = lb.at[:, my_tokens]
        return remote(part, part, xa_send.at[o], xa_recv.at[s], other("stripe", s, S, o))

    def gr_copy(o):
        to = lax.rem(m + o, G)
        return remote(gp.at[to], grs.at[m], gr_send.at[o], gr_recv.at[m], {"dp": zh * G + to})

    def gz_copy():
        return remote(gs, gz, gz_send, gz_recv, {"dp": pz})

    def ux_copy(o):
        return remote(ux.at[s], ux.at[s], ux_send.at[o], ux_recv.at[s], other("stripe", s, S, o))

    for o in range(1, G):
        fac_copy(p, o, {"dp": group_peer(o)}).start()

    def exchange():
        fac_copy(p, 0, {"dp": pz}).start()

    def forward():
        fac_copy(pz, 0, {"dp": pz}).wait_recv()
        for o in range(1, G):
            fac_copy(pz, G + o, {"dp": group_peer(o)}).start()

    def project():
        for o in range(1, G):
            fac_copy(zh * G + lax.rem(m + o, G), 0, {"dp": pz}).wait_recv()
            fac_copy((1 - zh) * G + lax.rem(m + o, G), 0, {"dp": pz}).wait_recv()
        loads[3].wait()
        last = s == S - 1
        zero = jnp.zeros((RANK, BLK), F32)

        @pl.loop(0, NB)
        def _(b):
            rows = pl.ds(pl.multiple_of(b * BLK, BLK), BLK)
            chosen = fac[ten_ref[0, b]]
            nt = (((1,), (1,)), ((), ()))
            low = lax.dot_general(chosen[:DOWN], xv[rows, :], nt, preferred_element_type=F32)
            grad = av[rows, quarter]
            first = lax.dot_general(chosen[DOWN:, :HALF], grad[:, :HALF], nt, preferred_element_type=F32)
            second = lax.dot_general(chosen[DOWN:, HALF:], grad[:, HALF:], nt, preferred_element_type=F32)
            both = jnp.concatenate(
                [
                    low,
                    jnp.where(last, zero, first + second),
                    jnp.where(last, first, zero),
                    jnp.where(last, second, zero),
                ],
                axis=0,
            )
            lp[:, rows] = (adapter_scale * both).astype(BF16)

        for o in range(1, S):
            xr_copy(o).start()

    def stripe_sum():
        total = lp[:, my_tokens].astype(F32)
        for o in range(1, S):
            src = lax.rem(s + o, S)
            remote(xs, xrs.at[src], xr_send.at[0], xr_recv.at[src], {"dp": pz}).wait_recv()
            total += xrs[src].astype(F32)
        xs[...] = total.astype(BF16)
        for g in range(6):

            @pl.when(t != owner(g))
            def _(g=g):
                zr_copy(g).start()

    def tensor_sum():
        for g in range(6):

            @pl.when(t == owner(g))
            def _(g=g):
                def add(o, total):
                    src = lax.rem(t + o, NT)
                    remote(
                        xs.at[section(g)], zrs.at[g, src], zr_send.at[g], zr_recv.at[g, src], {"dp": pz}
                    ).wait_recv()
                    return total + zrs[g, src].astype(F32)

                total = lax.fori_loop(1, NT, add, xs[section(g), :].astype(F32))
                lb[section(g), my_tokens] = total.astype(BF16)
                for o in range(1, NT):
                    za_copy(g, o).start()

    def stripe_spread():
        for g in range(6):

            @pl.when(t != owner(g))
            def _(g=g):
                za_copy(g, 1).wait_recv()

        for o in range(1, S):
            xa_copy(o).start()

    group = min(4, NP)

    def gradient():
        for o in range(1, S):
            src = lax.rem(s + o, S)
            part = lb.at[:, pl.ds(pl.multiple_of(src * QT, QT), QT)]
            remote(part, part, xa_send.at[0], xa_recv.at[src], {"dp": pz}).wait_recv()
        block_of = lax.div(lax.broadcasted_iota(jnp.int32, (1, TOK), 1), BLK)
        tenant = jnp.zeros((1, TOK), jnp.int32)
        for b in range(NB):
            tenant = jnp.where(block_of == b, ten_ref[0, b], tenant)
        last = s == S - 1
        sec_first = jnp.where(last, RANK, 0)
        sec_second = jnp.where(last, 2 * RANK, 0)

        @pl.loop(0, NP)
        def _(n):
            here = jnp.where(tenant == n, 1.0, 0.0).astype(BF16)
            gl[pl.ds(pl.multiple_of(n * DOWN, RANK), DOWN), :] = lb[pl.ds(DOWN, DOWN), :] * here
            rows = pl.ds(pl.multiple_of(n * RANK, RANK), RANK)
            ul[0, rows, :] = lb[pl.ds(pl.multiple_of(sec_first, RANK), RANK), :] * here
            ul[1, rows, :] = lb[pl.ds(pl.multiple_of(sec_second, RANK), RANK), :] * here

        @pl.loop(0, NP // group)
        def _(i):
            rows = pl.ds(pl.multiple_of(i * group * DOWN, RANK), group * DOWN)
            part = jnp.dot(gl[rows, :], xv[...], preferred_element_type=F32).astype(BF16)
            for e in range(group):
                n = i * group + e
                gp[lax.rem(n, G), lax.div(n, G), :DOWN, :] = part[e * DOWN : (e + 1) * DOWN]

        for h in range(2):
            lanes = pl.ds(pl.multiple_of(s * CQ + h * HALF, HALF), HALF)
            part = jnp.dot(ul[h], av[:, lanes], preferred_element_type=F32).astype(BF16)
            for n in range(NP):
                gp[n % G, n // G, DOWN:, h * HALF : (h + 1) * HALF] = part[n * RANK : (n + 1) * RANK]

        for o in range(1, G):
            gr_copy(o).start()

    def adapter():
        @pl.loop(0, NB)
        def _(b):
            rows = pl.ds(pl.multiple_of(b * BLK, BLK), BLK)
            down = fac[ten_ref[0, b]][:DOWN]
            extra = lax.dot_general(
                lb[pl.ds(DOWN, DOWN), rows], down, (((0,), (0,)), ((), ())), preferred_element_type=F32
            )
            acc[rows, :] = extra + pv[t, rows, :].astype(F32)

    def group_sum():
        for o in range(1, G):
            src = lax.rem(m + o, G)
            remote(gp.at[0], grs.at[src], gr_send.at[0], gr_recv.at[src], {"dp": pz}).wait_recv()

        def total(half):
            value = gp[m, half].astype(F32)
            for o in range(1, G):
                value += grs[lax.rem(m + o, G), half].astype(F32)
            return value

        gs[...] = total(1 - zh).astype(BF16)
        gz_copy().start()
        go[...] = total(zh)

    def half_sum():
        gz_copy().wait_recv()
        grad = go[...] + gz[...].astype(F32)
        ux[s] = grad[DOWN:]
        for o in range(1, S):
            ux_copy(o).start()
        for load in loads[4:]:
            load.wait()
        dnn[...], dmv[...], dvv[...] = adam(fac[p, :DOWN, :], dmv[...], dvv[...], grad[:DOWN])
        for store in stores[:3]:
            store.start()

    def up_adam():
        for o in range(1, S):
            src = lax.rem(s + o, S)
            remote(ux.at[src], ux.at[src], ux_send.at[0], ux_recv.at[src], {"dp": pz}).wait_recv()
        for i in range(S):
            lanes = pl.ds(i * CQ, CQ)
            upn[:, lanes], umv[:, lanes], uvv[:, lanes] = adam(
                upv[:, lanes], umv[:, lanes], uvv[:, lanes], ux[i]
            )
        for store in stores[3:]:
            store.start()

    stores = [
        pltpu.make_async_copy(dnn, dn_o.at[0], store_sem.at[0]),
        pltpu.make_async_copy(dmv, dm_o.at[0], store_sem.at[1]),
        pltpu.make_async_copy(dvv, dv_o.at[0], store_sem.at[2]),
        pltpu.make_async_copy(upn, up_o.at[0], store_sem.at[3]),
        pltpu.make_async_copy(umv, um_o.at[0], store_sem.at[4]),
        pltpu.make_async_copy(uvv, uv_o.at[0], store_sem.at[5]),
    ]

    def rank(way):
        return t if way == 0 else NT - 1 - t

    def line_copy(way, u):
        k, q = lax.div(u, PIECES), lax.rem(u, PIECES)
        j = NT - 1 - k if way == 0 else k
        rows = pl.ds(pl.multiple_of(q * PR, PR), PR)
        to = t + 1 if way == 0 else t - 1
        return j, rows, remote(
            pv.at[j, rows], rv.at[way, j, rows], line_send.at[j, q], line_recv.at[way, j, q], {"tensor": to}
        )

    def line_step(v):
        for way in range(2):
            r = rank(way)
            u = v - SKEW * r

            @pl.when((u >= 0) & (u < (NT - 1 - r) * PIECES))
            def _(way=way, r=r, u=u):
                j, rows, copy = line_copy(way, u)

                @pl.when(r > 0)
                def _():
                    copy.wait_recv()
                    pv[j, rows, :] = (pv[j, rows, :].astype(F32) + rv[way, j, rows, :].astype(F32)).astype(BF16)

                @pl.when(u >= AHEAD)
                def _():
                    line_copy(way, u - AHEAD)[2].wait_send()

                copy.start()

    greetings = range(1, NT)
    stages = [(AT_GREET + (slot + 0) // 2, functools.partial(greet, slot)) for slot in greetings]
    stages += [
        (AT_EXCHANGE, exchange),
        (AT_FORWARD, forward),
        (AT_PROJECT, project),
        (AT_STRIPE_SUM, stripe_sum),
        (AT_TENSOR_SUM, tensor_sum),
        (AT_STRIPE_SPREAD, stripe_spread),
        (AT_GRADIENT, gradient),
        (AT_ADAPTER, adapter),
        (AT_GROUP_SUM, group_sum),
        (AT_HALF_SUM, half_sum),
        (AT_UP_ADAM, up_adam),
    ]
    steps = max((NT - 1 - r) * PIECES + SKEW * r for r in range(NT - 1))
    steps = max(steps, AT_UP_ADAM + 1, NT)

    @pl.loop(0, steps)
    def _(v):
        line_step(v)

        @pl.when(v < NT - 1)
        def _():
            multiply(v + 1)

        for at, stage in stages:
            pl.when(v == at)(stage)

    def finish(q):
        rows = pl.ds(q * PR, PR)
        for way in range(2):

            @pl.when(rank(way) > 0)
            def _(way=way):
                part = rv.at[way, t, rows]
                remote(part, part, line_send.at[t, q], line_recv.at[way, t, q], {"dp": pz}).wait_recv()
                acc[rows, :] += rv[way, t, rows, :].astype(F32)

        ov[rows, :] = acc[rows, :].astype(BF16)
        return pltpu.make_async_copy(ov.at[rows], out_o.at[rows], out_sem.at[q])

    writes = []
    for q in range(PIECES):
        write = finish(q)
        write.start()
        writes.append(write)

    for way in range(2):
        r = rank(way)

        @pl.when(r < NT - 1)
        def _(way=way, r=r):
            for back in range(AHEAD):
                line_copy(way, (NT - 1 - r) * PIECES - AHEAD + back)[2].wait_send()

    fac_copy(p, 0, {"dp": pz}).wait_send()
    for o in range(1, G):
        fac_copy(p, o, {"dp": group_peer(o)}).wait_send()
        fac_copy(pz, G + o, {"dp": group_peer(o)}).wait_send()
        gr_copy(o).wait_send()
    for o in range(1, S):
        xr_copy(o).wait_send()
        xa_copy(o).wait_send()
        ux_copy(o).wait_send()
    for g in range(6):

        @pl.when(t != owner(g))
        def _(g=g):
            zr_copy(g).wait_send()

        @pl.when(t == owner(g))
        def _(g=g):
            for o in range(1, NT):
                za_copy(g, o).wait_send()

    gz_copy().wait_send()
    for store in stores:
        store.wait()
    for write in writes:
        write.wait()


def deliver(*refs):
    ins, outs, held, (sems,) = refs[:7], refs[7:14], refs[14:21], refs[21:]
    copies = [pltpu.make_async_copy(ins[i], held[i], sems.at[i]) for i in range(7)]
    for copy in copies:
        copy.start()
    writes = [pltpu.make_async_copy(held[i], outs[i], sems.at[7 + i]) for i in range(7)]
    for copy, write in zip(copies, writes):
        copy.wait()
        write.start()
    for write in writes:
        write.wait()


def on_device(
    S, NP, NT,
    normed_layer_input,
    projection_output_gradient,
    frozen_projection_weight,
    block_owner_tenant,
    block_token_fill,
    adapter_down_factors,
    down_first_moment,
    down_second_moment,
    adapter_up_factors,
    up_first_moment,
    up_second_moment,
):
    tok, d = normed_layer_input.shape
    c = projection_output_gradient.shape[1]
    w_rows = frozen_projection_weight.shape[0]
    G = NP // 2
    qt = tok // S
    any_space = pl.BlockSpec(memory_space=pl.ANY)
    hbm = pl.BlockSpec(memory_space=pltpu.HBM)
    smem = pl.BlockSpec(memory_space=pltpu.SMEM)
    outs = (
        jax.ShapeDtypeStruct((tok, d), BF16),
        jax.ShapeDtypeStruct(adapter_down_factors.shape, BF16),
        jax.ShapeDtypeStruct(down_first_moment.shape, F32),
        jax.ShapeDtypeStruct(down_second_moment.shape, F32),
        jax.ShapeDtypeStruct(adapter_up_factors.shape, BF16),
        jax.ShapeDtypeStruct(up_first_moment.shape, F32),
        jax.ShapeDtypeStruct(up_second_moment.shape, F32),
    )
    vm, dma = pltpu.VMEM, pltpu.SemaphoreType.DMA
    scratch = [
        vm((tok, c), BF16),
        vm((w_rows, c), BF16),
        vm((tok, d), BF16),
        vm((NP, FAC, d), BF16),
        vm((NT, tok, w_rows // NT), BF16),
        vm((2, NT, tok, w_rows // NT), BF16),
        vm((2 * DOWN, tok), BF16),
        vm((S, 2 * DOWN, qt), BF16),
        vm((2 * DOWN, qt), BF16),
        vm((6, NT, RANK, qt), BF16),
        vm((2 * DOWN, tok), BF16),
        vm((NP * DOWN, tok), BF16),
        vm((2, NP * RANK, tok), BF16),
        vm((G, 2, FAC, d), BF16),
        vm((G, 2, FAC, d), BF16),
        vm((FAC, d), F32),
        vm((FAC, d), BF16),
        vm((FAC, d), BF16),
        vm((S, RANK, c // S), F32),
        vm((tok, d), F32),
        vm((tok, d), BF16),
        vm((DOWN, d), F32),
        vm((DOWN, d), F32),
        vm((RANK, c), F32),
        vm((RANK, c), F32),
        vm((RANK, c), BF16),
        vm((DOWN, d), BF16),
        vm((RANK, c), BF16),
        dma((9,)), dma((NT,)), dma((PIECES,)), dma((6,)),
        dma((NT, PIECES)), dma((2, NT, PIECES)),
        dma((2 * G,)), dma((NP,)),
        dma((S,)), dma((S,)), dma((6,)), dma((6, NT)), dma((6, NT)), dma((6,)), dma((S,)), dma((S,)),
        dma((G,)), dma((G,)), dma, dma, dma((S,)), dma((S,)), pltpu.SemaphoreType.REGULAR((2, NT)),
    ]
    results = pl.pallas_call(
        functools.partial(kernel, S, NP, NT),
        out_shape=outs,
        in_specs=[smem] * 2 + [hbm] * 9,
        out_specs=[any_space] * 7,
        scratch_shapes=scratch,
        compiler_params=pltpu.CompilerParams(
            collective_id=0, has_side_effects=True, vmem_limit_bytes=VMEM_BYTES
        ),
        cost_estimate=pl.CostEstimate(
            flops=2 * tok * c * w_rows, bytes_accessed=2 * (tok * c + w_rows * c), transcendentals=0
        ),
        name="united_backward",
    )(
        block_owner_tenant.T,
        block_token_fill.T,
        normed_layer_input,
        projection_output_gradient,
        frozen_projection_weight,
        adapter_down_factors,
        down_first_moment,
        down_second_moment,
        adapter_up_factors,
        up_first_moment,
        up_second_moment,
    )
    return pl.pallas_call(
        deliver,
        out_shape=outs,
        in_specs=[any_space] * 7,
        out_specs=[hbm] * 7,
        scratch_shapes=[vm(out.shape, out.dtype) for out in outs] + [dma((14,))],
        compiler_params=pltpu.CompilerParams(vmem_limit_bytes=VMEM_BYTES),
        name="deliver",
    )(*results)


def solution(mesh):
    both = ("stripe", "tensor")
    return jax.shard_map(
        functools.partial(on_device, mesh.shape["stripe"], mesh.shape["dp"], mesh.shape["tensor"]),
        mesh=mesh,
        in_specs=(
            P("dp", both),
            P("dp", "tensor"),
            P("stripe", "tensor"),
            P("dp", None),
            P("dp", None),
            P("dp", None, both),
            P("dp", None, both),
            P("dp", None, both),
            P("dp", None, "tensor"),
            P("dp", None, "tensor"),
            P("dp", None, "tensor"),
        ),
        out_specs=(
            P("dp", both),
            P("dp", None, both),
            P("dp", None, both),
            P("dp", None, both),
            P("dp", None, "tensor"),
            P("dp", None, "tensor"),
            P("dp", None, "tensor"),
        ),
        check_vma=False,
    )
```

```python
import functools

import jax
import jax.numpy as jnp
from jax import lax
from jax.experimental import pallas as pl
from jax.experimental.pallas import tpu as pltpu
from jax.sharding import PartitionSpec as P

BLK = 128
RANK = 16
DOWN = 48
FAC = 64
PIECES = 4
SKEW = 2
AHEAD = 4
VMEM_BYTES = 62 * 1024 * 1024

adapter_scale = 2.0
beta_one = 0.9
beta_two = 0.95
adam_rate = 0.001
adam_eps = 1e-08
adam_steps = 10.0

F32 = jnp.float32
BF16 = jnp.bfloat16
MESH = pl.DeviceIdType.MESH

AT_GREET = 0
AT_EXCHANGE = 1
AT_RELAY = 3
AT_FORWARD = 5
AT_PROJECT = 8
AT_STRIPE_SUM = 10
AT_TENSOR_SUM = 12
AT_STRIPE_SPREAD = 15
AT_GRADIENT = 17
AT_ADAPTER = 18
AT_GROUP_SUM = 20
AT_OWN_SUM = 21
AT_RELAY_SUM = 22
AT_HALF_SUM = 25
AT_UP_ADAM = 27


def adam(params, moment, second, gradient):
    moment_new = beta_one * moment + (1.0 - beta_one) * gradient
    second_new = beta_two * second + (1.0 - beta_two) * (gradient * gradient)
    first_fix = moment_new / (1.0 - beta_one**adam_steps)
    second_fix = second_new / (1.0 - beta_two**adam_steps)
    stepped = params.astype(F32) - adam_rate * first_fix / (jnp.sqrt(second_fix) + adam_eps)
    return stepped.astype(BF16), moment_new, second_new


def kernel(
    S, NP, NT,
    ten_ref, fill_ref,
    x_in, a_in, w_in, dn_in, dm_in, dv_in, up_in, um_in, uv_in,
    out_o, dn_o, dm_o, dv_o, up_o, um_o, uv_o,
    av, wv, xv, fac, pv, rv,
    lp, xrs, xs, zrs, lb, fac_held, sum_held,
    gl, ul, gp, grs, go, gs, gz, ux, acc, ov,
    dmv, dvv, umv, uvv, upv, dnn, upn,
    load_sem, a_sem, w_sem, out_sem, store_sem,
    line_send, line_recv,
    fac_send, fac_recv,
    xr_send, xr_recv, zr_send, zr_recv, za_send, za_recv, xa_send, xa_recv,
    gr_send, gr_recv, gz_send, gz_recv, ux_send, ux_recv, hello,
    out_send, relay_send, relay_recv,
):
    G = NP // 2
    TOK, C = av.shape
    D = xv.shape[1]
    NB = TOK // BLK
    QT = TOK // S
    CQ = C // S
    HALF = CQ // 2
    PR = TOK // PIECES
    CHUNK = wv.shape[0] // NT
    s = lax.axis_index("stripe")
    p = lax.axis_index("dp")
    t = lax.axis_index("tensor")
    zh = lax.div(p, G)
    m = lax.rem(p, G)
    pz = (1 - zh) * G + m

    def remote(src, dst, send, recv, device):
        return pltpu.make_async_remote_copy(
            src_ref=src, dst_ref=dst, send_sem=send, recv_sem=recv, device_id=device, device_id_type=MESH
        )

    def other(axis, here, size, o):
        return {axis: lax.rem(here + o, size)}

    def group_peer(o):
        return zh * G + lax.rem(m + o, G)

    quarter = pl.ds(pl.multiple_of(s * CQ, CQ), CQ)
    my_tokens = pl.ds(pl.multiple_of(s * QT, QT), QT)
    loads = [
        pltpu.make_async_copy(dn_in.at[0], fac.at[p, pl.ds(0, DOWN)], load_sem.at[0]),
        pltpu.make_async_copy(up_in.at[0, :, quarter], fac.at[p, pl.ds(DOWN, RANK)], load_sem.at[1]),
        pltpu.make_async_copy(x_in, xv, load_sem.at[2]),
        pltpu.make_async_copy(dm_in.at[0], dmv, load_sem.at[3]),
        pltpu.make_async_copy(dv_in.at[0], dvv, load_sem.at[4]),
        pltpu.make_async_copy(um_in.at[0], umv, load_sem.at[5]),
        pltpu.make_async_copy(uv_in.at[0], uvv, load_sem.at[6]),
        pltpu.make_async_copy(up_in.at[0], upv, load_sem.at[7]),
    ]

    def order(i):
        inner = jnp.where(lax.rem(i, 2) == 0, NT - 1 - lax.div(i, 2), lax.div(i, 2))
        return jnp.where(t == 0, NT - 1 - i, jnp.where(t == NT - 1, i, inner))

    def w_load(j):
        rows = pl.ds(pl.multiple_of(j * CHUNK, CHUNK), CHUNK)
        return pltpu.make_async_copy(w_in.at[rows], wv.at[rows], w_sem.at[j])

    def a_load(q):
        rows = pl.ds(q * PR, PR)
        return pltpu.make_async_copy(a_in.at[rows], av.at[rows], a_sem.at[q])

    a_load(0).start()
    w_load(order(jnp.int32(0))).start()
    for load in loads[:2]:
        load.start()
    for q in range(1, PIECES):
        a_load(q).start()
    for i in range(1, NT):
        w_load(order(jnp.int32(i))).start()
    for load in loads[2:]:
        load.start()

    z = zh * NT + t
    after = {"dp": jnp.where(t == NT - 1, p + G, p), "tensor": lax.rem(t + 1, NT)}
    before = {"dp": jnp.where(t == 0, p - G, p), "tensor": lax.rem(t + NT - 1, NT)}
    has_after, has_before = z < 2 * NT - 1, z > 0
    barrier = pltpu.get_barrier_semaphore()
    partners = [other("stripe", s, S, o) for o in range(1, S)]
    partners += [{"dp": group_peer(o)} for o in range(1, G)]
    for partner in partners:
        pl.semaphore_signal(barrier, inc=1, device_id=partner, device_id_type=MESH)
    for there, partner in ((has_after, after), (has_before, before)):

        @pl.when(there)
        def _(partner=partner):
            pl.semaphore_signal(barrier, inc=1, device_id=partner, device_id_type=MESH)

    def multiply(i):
        j = order(i)
        w_load(j).wait()
        part = lax.dot_general(
            av[...],
            wv[pl.ds(pl.multiple_of(j * CHUNK, CHUNK), CHUNK), :],
            (((1,), (1,)), ((), ())),
            preferred_element_type=F32,
        )
        pv[j] = part.astype(BF16)

    def begin(q):
        a_load(q).wait()

        @pl.loop(q * PR // BLK, (q + 1) * PR // BLK)
        def _(b):
            rows = pl.ds(pl.multiple_of(b * BLK, BLK), BLK)
            place = lax.broadcasted_iota(jnp.int32, (BLK, C), 0)
            block = av[rows, :]
            av[rows, :] = jnp.where(place < fill_ref[0, b], block, jnp.zeros_like(block))

        j = order(jnp.int32(0))
        if q == 0:
            w_load(j).wait()
        rows = pl.ds(q * PR, PR)
        part = lax.dot_general(
            av[rows, :],
            wv[pl.ds(pl.multiple_of(j * CHUNK, CHUNK), CHUNK), :],
            (((1,), (1,)), ((), ())),
            preferred_element_type=F32,
        )
        pv[j, rows, :] = part.astype(BF16)

    begin(0)
    loads[0].wait()
    loads[1].wait()
    pl.semaphore_wait(barrier, len(partners) + jnp.where(has_after & has_before, 2, 1))

    def greet(slot):
        for way, to, there in ((0, after, has_after), (1, before, has_before)):
            r = z if way == 0 else 2 * NT - 1 - z
            if slot >= 1:

                @pl.when(r >= slot + 1)
                def _(way=way):
                    pl.semaphore_wait(hello.at[way, slot], 1)

            if slot + 1 < NT - 1:

                @pl.when((r >= slot + 1) & there)
                def _(way=way, to=to):
                    pl.semaphore_signal(hello.at[way, slot + 1], inc=1, device_id=to, device_id_type=MESH)

    def rank(way):
        return t if way == 0 else NT - 1 - t

    def line_copy(way, u):
        k, q = lax.div(u, PIECES), lax.rem(u, PIECES)
        j = NT - 1 - k if way == 0 else k
        rows = pl.ds(pl.multiple_of(q * PR, PR), PR)
        to = t + 1 if way == 0 else t - 1
        return j, rows, remote(
            pv.at[j, rows], rv.at[way, j, rows], line_send.at[j, q], line_recv.at[way, j, q], {"tensor": to}
        )

    def line_step(v):
        for way in range(2):
            r = rank(way)
            u = v - SKEW * r

            @pl.when((u >= 0) & (u < (NT - 1 - r) * PIECES))
            def _(way=way, r=r, u=u):
                j, rows, copy = line_copy(way, u)

                @pl.when(r > 0)
                def _():
                    copy.wait_recv()
                    pv[j, rows, :] = (pv[j, rows, :].astype(F32) + rv[way, j, rows, :].astype(F32)).astype(BF16)

                @pl.when(u >= AHEAD)
                def _():
                    line_copy(way, u - AHEAD)[2].wait_send()

                copy.start()

    greet(0)
    line_step(jnp.int32(0))

    def fac_copy(slot, i, device):
        return remote(fac.at[slot], fac.at[slot], fac_send.at[i], fac_recv.at[slot], device)

    def xr_copy(o):
        to = lax.rem(s + o, S)
        lanes = pl.ds(pl.multiple_of(to * QT, QT), QT)
        return remote(lp.at[:, lanes], xrs.at[s], xr_send.at[o], xr_recv.at[s], {"stripe": to})

    def owner(g):
        return (g + 1) % NT

    def section(g):
        return pl.ds(g * RANK, RANK)

    def zr_copy(g):
        return remote(xs.at[section(g)], zrs.at[g, t], zr_send.at[g], zr_recv.at[g, t], {"tensor": owner(g)})

    def za_copy(g, o):
        part = lb.at[section(g), my_tokens]
        return remote(part, part, za_send.at[g, o], za_recv.at[g], other("tensor", t, NT, o))

    def xa_copy(o):
        part = lb.at[:, my_tokens]
        return remote(part, part, xa_send.at[o], xa_recv.at[s], other("stripe", s, S, o))

    def gr_copy(o, half):
        to = lax.rem(m + o, G)
        return remote(
            gp.at[to, half], grs.at[m, half], gr_send.at[o, half], gr_recv.at[m, half], {"dp": zh * G + to}
        )

    MID = NT // 2
    far = lax.rem(t + MID, NT)
    half_way = {"dp": jnp.where(t < MID, m, G + m), "tensor": far}
    is_relay = (z >= MID) & (z < NT + MID)

    def to_relay(src, buf, i):
        return remote(src, buf.at[zh], out_send.at[i], relay_recv.at[i, zh], half_way)

    def from_relay(buf, dst, i, side, recv):
        return remote(
            buf.at[side], dst, relay_send.at[i, side], recv, {"dp": (1 - side) * G + m, "tensor": far}
        )

    def fac_relay(side):
        slot = side * G + m
        return from_relay(fac_held, fac.at[slot], 0, side, fac_recv.at[slot])

    def sum_relay(side):
        return from_relay(sum_held, gz, 1, side, gz_recv)

    def ux_copy(o):
        return remote(ux.at[s], ux.at[s], ux_send.at[o], ux_recv.at[s], other("stripe", s, S, o))

    for o in range(1, G):
        fac_copy(p, o, {"dp": group_peer(o)}).start()

    for q in range(1, PIECES):
        begin(q)
    greet(1)

    def exchange():
        to_relay(fac.at[p], fac_held, 0).start()

    def relay():
        @pl.when(is_relay)
        def _():
            for side in range(2):
                remote(gs, fac_held.at[side], gz_send, relay_recv.at[0, side], {"dp": pz}).wait_recv()
                fac_relay(side).start()

    def relay_sum():
        @pl.when(is_relay)
        def _():
            for side in range(2):
                remote(gs, sum_held.at[side], gz_send, relay_recv.at[1, side], {"dp": pz}).wait_recv()
                sum_relay(side).start()

    def forward():
        fac_copy(pz, 0, {"dp": pz}).wait_recv()
        for o in range(1, G):
            fac_copy(pz, G + o, {"dp": group_peer(o)}).start()

    def project():
        for o in range(1, G):
            fac_copy(zh * G + lax.rem(m + o, G), 0, {"dp": pz}).wait_recv()
            fac_copy((1 - zh) * G + lax.rem(m + o, G), 0, {"dp": pz}).wait_recv()
        loads[2].wait()
        last = s == S - 1
        zero = jnp.zeros((RANK, BLK), F32)

        @pl.loop(0, NB)
        def _(b):
            rows = pl.ds(pl.multiple_of(b * BLK, BLK), BLK)
            chosen = fac[ten_ref[0, b]]
            nt = (((1,), (1,)), ((), ()))
            low = lax.dot_general(chosen[:DOWN], xv[rows, :], nt, preferred_element_type=F32)
            grad = av[rows, quarter]
            first = lax.dot_general(chosen[DOWN:, :HALF], grad[:, :HALF], nt, preferred_element_type=F32)
            second = lax.dot_general(chosen[DOWN:, HALF:], grad[:, HALF:], nt, preferred_element_type=F32)
            both = jnp.concatenate(
                [
                    low,
                    jnp.where(last, zero, first + second),
                    jnp.where(last, first, zero),
                    jnp.where(last, second, zero),
                ],
                axis=0,
            )
            lp[:, rows] = (adapter_scale * both).astype(BF16)

        for o in range(1, S):
            xr_copy(o).start()

    def stripe_sum():
        total = lp[:, my_tokens].astype(F32)
        for o in range(1, S):
            src = lax.rem(s + o, S)
            remote(xs, xrs.at[src], xr_send.at[0], xr_recv.at[src], {"dp": pz}).wait_recv()
            total += xrs[src].astype(F32)
        xs[...] = total.astype(BF16)
        for g in range(6):

            @pl.when(t != owner(g))
            def _(g=g):
                zr_copy(g).start()

    def tensor_sum():
        for g in range(6):

            @pl.when(t == owner(g))
            def _(g=g):
                def add(o, total):
                    src = lax.rem(t + o, NT)
                    remote(
                        xs.at[section(g)], zrs.at[g, src], zr_send.at[g], zr_recv.at[g, src], {"dp": pz}
                    ).wait_recv()
                    return total + zrs[g, src].astype(F32)

                total = lax.fori_loop(1, NT, add, xs[section(g), :].astype(F32))
                lb[section(g), my_tokens] = total.astype(BF16)
                for o in range(1, NT):
                    za_copy(g, o).start()

    def stripe_spread():
        for g in range(6):

            @pl.when(t != owner(g))
            def _(g=g):
                za_copy(g, 1).wait_recv()

        for o in range(1, S):
            xa_copy(o).start()

    group = min(4, NP)

    def gradient():
        for o in range(1, S):
            src = lax.rem(s + o, S)
            part = lb.at[:, pl.ds(pl.multiple_of(src * QT, QT), QT)]
            remote(part, part, xa_send.at[0], xa_recv.at[src], {"dp": pz}).wait_recv()
        block_of = lax.div(lax.broadcasted_iota(jnp.int32, (1, TOK), 1), BLK)
        tenant = jnp.zeros((1, TOK), jnp.int32)
        for b in range(NB):
            tenant = jnp.where(block_of == b, ten_ref[0, b], tenant)
        last = s == S - 1
        sec_first = jnp.where(last, RANK, 0)
        sec_second = jnp.where(last, 2 * RANK, 0)

        @pl.loop(0, NP)
        def _(n):
            here = jnp.where(tenant == n, 1.0, 0.0).astype(BF16)
            gl[pl.ds(pl.multiple_of(n * DOWN, RANK), DOWN), :] = lb[pl.ds(DOWN, DOWN), :] * here
            rows = pl.ds(pl.multiple_of(n * RANK, RANK), RANK)
            ul[0, rows, :] = lb[pl.ds(pl.multiple_of(sec_first, RANK), RANK), :] * here
            ul[1, rows, :] = lb[pl.ds(pl.multiple_of(sec_second, RANK), RANK), :] * here

        @pl.loop(0, NP // group)
        def _(i):
            rows = pl.ds(pl.multiple_of(i * group * DOWN, RANK), group * DOWN)
            part = jnp.dot(gl[rows, :], xv[...], preferred_element_type=F32).astype(BF16)
            for e in range(group):
                n = i * group + e
                gp[lax.rem(n, G), lax.div(n, G), :DOWN, :] = part[e * DOWN : (e + 1) * DOWN]

        for h in range(2):
            lanes = pl.ds(pl.multiple_of(s * CQ + h * HALF, HALF), HALF)
            part = jnp.dot(ul[h], av[:, lanes], preferred_element_type=F32).astype(BF16)
            for n in range(NP):
                gp[n % G, n // G, DOWN:, h * HALF : (h + 1) * HALF] = part[n * RANK : (n + 1) * RANK]

        for half in (1 - zh, zh):
            for o in range(1, G):
                gr_copy(o, half).start()

    def adapter():
        @pl.loop(0, NB)
        def _(b):
            rows = pl.ds(pl.multiple_of(b * BLK, BLK), BLK)
            down = fac[ten_ref[0, b]][:DOWN]
            extra = lax.dot_general(
                lb[pl.ds(DOWN, DOWN), rows], down, (((0,), (0,)), ((), ())), preferred_element_type=F32
            )
            acc[rows, :] = extra + pv[t, rows, :].astype(F32)

    def total(half):
        value = gp[m, half].astype(F32)
        for o in range(1, G):
            src = lax.rem(m + o, G)
            remote(
                gp.at[0, half], grs.at[src, half], gr_send.at[0, half], gr_recv.at[src, half], {"dp": pz}
            ).wait_recv()
            value += grs[src, half].astype(F32)
        return value

    def group_sum():
        gs[...] = total(1 - zh).astype(BF16)
        to_relay(gs, sum_held, 1).start()

    def own_sum():
        go[...] = total(zh)

    def half_sum():
        remote(gs, gz, gz_send, gz_recv, {"dp": pz}).wait_recv()
        grad = go[...] + gz[...].astype(F32)
        ux[s] = grad[DOWN:]
        for o in range(1, S):
            ux_copy(o).start()
        for load in loads[3:]:
            load.wait()
        dnn[...], dmv[...], dvv[...] = adam(fac[p, :DOWN, :], dmv[...], dvv[...], grad[:DOWN])
        for store in stores[:3]:
            store.start()

    def up_adam():
        for o in range(1, S):
            src = lax.rem(s + o, S)
            remote(ux.at[src], ux.at[src], ux_send.at[0], ux_recv.at[src], {"dp": pz}).wait_recv()
        for i in range(S):
            lanes = pl.ds(i * CQ, CQ)
            upn[:, lanes], umv[:, lanes], uvv[:, lanes] = adam(
                upv[:, lanes], umv[:, lanes], uvv[:, lanes], ux[i]
            )
        for store in stores[3:]:
            store.start()

    stores = [
        pltpu.make_async_copy(dnn, dn_o.at[0], store_sem.at[0]),
        pltpu.make_async_copy(dmv, dm_o.at[0], store_sem.at[1]),
        pltpu.make_async_copy(dvv, dv_o.at[0], store_sem.at[2]),
        pltpu.make_async_copy(upn, up_o.at[0], store_sem.at[3]),
        pltpu.make_async_copy(umv, um_o.at[0], store_sem.at[4]),
        pltpu.make_async_copy(uvv, uv_o.at[0], store_sem.at[5]),
    ]

    greetings = range(2, NT - 1)
    stages = [(AT_GREET + slot // 2, functools.partial(greet, slot)) for slot in greetings]
    stages += [
        (AT_EXCHANGE, exchange),
        (AT_RELAY, relay),
        (AT_FORWARD, forward),
        (AT_PROJECT, project),
        (AT_STRIPE_SUM, stripe_sum),
        (AT_TENSOR_SUM, tensor_sum),
        (AT_STRIPE_SPREAD, stripe_spread),
        (AT_GRADIENT, gradient),
        (AT_ADAPTER, adapter),
        (AT_GROUP_SUM, group_sum),
        (AT_OWN_SUM, own_sum),
        (AT_RELAY_SUM, relay_sum),
        (AT_HALF_SUM, half_sum),
        (AT_UP_ADAM, up_adam),
    ]
    steps = max((NT - 1 - r) * PIECES + SKEW * r for r in range(NT - 1))
    steps = max(steps, AT_UP_ADAM + 1, NT)

    @pl.loop(1, steps)
    def _(v):
        line_step(v)

        @pl.when(v < NT)
        def _():
            multiply(v)

        for at, stage in stages:
            pl.when(v == at)(stage)

    def finish(q):
        rows = pl.ds(q * PR, PR)
        for way in range(2):

            @pl.when(rank(way) > 0)
            def _(way=way):
                part = rv.at[way, t, rows]
                remote(part, part, line_send.at[t, q], line_recv.at[way, t, q], {"dp": pz}).wait_recv()
                acc[rows, :] += rv[way, t, rows, :].astype(F32)

        ov[rows, :] = acc[rows, :].astype(BF16)
        return pltpu.make_async_copy(ov.at[rows], out_o.at[rows], out_sem.at[q])

    writes = []
    for q in range(PIECES):
        write = finish(q)
        write.start()
        writes.append(write)

    for way in range(2):
        r = rank(way)

        @pl.when(r < NT - 1)
        def _(way=way, r=r):
            for back in range(AHEAD):
                line_copy(way, (NT - 1 - r) * PIECES - AHEAD + back)[2].wait_send()

    for o in range(1, G):
        fac_copy(p, o, {"dp": group_peer(o)}).wait_send()
        fac_copy(pz, G + o, {"dp": group_peer(o)}).wait_send()
        gr_copy(o, 0).wait_send()
        gr_copy(o, 1).wait_send()
    for o in range(1, S):
        xr_copy(o).wait_send()
        xa_copy(o).wait_send()
        ux_copy(o).wait_send()
    for g in range(6):

        @pl.when(t != owner(g))
        def _(g=g):
            zr_copy(g).wait_send()

        @pl.when(t == owner(g))
        def _(g=g):
            for o in range(1, NT):
                za_copy(g, o).wait_send()

    to_relay(fac.at[p], fac_held, 0).wait_send()
    to_relay(gs, sum_held, 1).wait_send()

    @pl.when(is_relay)
    def _():
        for side in range(2):
            fac_relay(side).wait_send()
            sum_relay(side).wait_send()

    for store in stores:
        store.wait()
    for write in writes:
        write.wait()


def deliver(*refs):
    ins, outs, held, (sems,) = refs[:7], refs[7:14], refs[14:21], refs[21:]
    copies = [pltpu.make_async_copy(ins[i], held[i], sems.at[i]) for i in range(7)]
    for copy in copies:
        copy.start()
    writes = [pltpu.make_async_copy(held[i], outs[i], sems.at[7 + i]) for i in range(7)]
    for copy, write in zip(copies, writes):
        copy.wait()
        write.start()
    for write in writes:
        write.wait()


def on_device(
    S, NP, NT,
    normed_layer_input,
    projection_output_gradient,
    frozen_projection_weight,
    block_owner_tenant,
    block_token_fill,
    adapter_down_factors,
    down_first_moment,
    down_second_moment,
    adapter_up_factors,
    up_first_moment,
    up_second_moment,
):
    tok, d = normed_layer_input.shape
    c = projection_output_gradient.shape[1]
    w_rows = frozen_projection_weight.shape[0]
    G = NP // 2
    qt = tok // S
    any_space = pl.BlockSpec(memory_space=pl.ANY)
    hbm = pl.BlockSpec(memory_space=pltpu.HBM)
    smem = pl.BlockSpec(memory_space=pltpu.SMEM)
    outs = (
        jax.ShapeDtypeStruct((tok, d), BF16),
        jax.ShapeDtypeStruct(adapter_down_factors.shape, BF16),
        jax.ShapeDtypeStruct(down_first_moment.shape, F32),
        jax.ShapeDtypeStruct(down_second_moment.shape, F32),
        jax.ShapeDtypeStruct(adapter_up_factors.shape, BF16),
        jax.ShapeDtypeStruct(up_first_moment.shape, F32),
        jax.ShapeDtypeStruct(up_second_moment.shape, F32),
    )
    vm, dma = pltpu.VMEM, pltpu.SemaphoreType.DMA
    scratch = [
        vm((tok, c), BF16),
        vm((w_rows, c), BF16),
        vm((tok, d), BF16),
        vm((NP, FAC, d), BF16),
        vm((NT, tok, w_rows // NT), BF16),
        vm((2, NT, tok, w_rows // NT), BF16),
        vm((2 * DOWN, tok), BF16),
        vm((S, 2 * DOWN, qt), BF16),
        vm((2 * DOWN, qt), BF16),
        vm((6, NT, RANK, qt), BF16),
        vm((2 * DOWN, tok), BF16),
        vm((2, FAC, d), BF16),
        vm((2, FAC, d), BF16),
        vm((NP * DOWN, tok), BF16),
        vm((2, NP * RANK, tok), BF16),
        vm((G, 2, FAC, d), BF16),
        vm((G, 2, FAC, d), BF16),
        vm((FAC, d), F32),
        vm((FAC, d), BF16),
        vm((FAC, d), BF16),
        vm((S, RANK, c // S), F32),
        vm((tok, d), F32),
        vm((tok, d), BF16),
        vm((DOWN, d), F32),
        vm((DOWN, d), F32),
        vm((RANK, c), F32),
        vm((RANK, c), F32),
        vm((RANK, c), BF16),
        vm((DOWN, d), BF16),
        vm((RANK, c), BF16),
        dma((8,)), dma((PIECES,)), dma((NT,)), dma((PIECES,)), dma((6,)),
        dma((NT, PIECES)), dma((2, NT, PIECES)),
        dma((2 * G,)), dma((NP,)),
        dma((S,)), dma((S,)), dma((6,)), dma((6, NT)), dma((6, NT)), dma((6,)), dma((S,)), dma((S,)),
        dma((G, 2)), dma((G, 2)), dma, dma, dma((S,)), dma((S,)), pltpu.SemaphoreType.REGULAR((2, NT)),
        dma((2,)), dma((2, 2)), dma((2, 2)),
    ]
    results = pl.pallas_call(
        functools.partial(kernel, S, NP, NT),
        out_shape=outs,
        in_specs=[smem] * 2 + [hbm] * 9,
        out_specs=[any_space] * 7,
        scratch_shapes=scratch,
        compiler_params=pltpu.CompilerParams(
            collective_id=0, has_side_effects=True, vmem_limit_bytes=VMEM_BYTES
        ),
        cost_estimate=pl.CostEstimate(
            flops=2 * tok * c * w_rows, bytes_accessed=2 * (tok * c + w_rows * c), transcendentals=0
        ),
        name="united_backward",
    )(
        block_owner_tenant.T,
        block_token_fill.T,
        normed_layer_input,
        projection_output_gradient,
        frozen_projection_weight,
        adapter_down_factors,
        down_first_moment,
        down_second_moment,
        adapter_up_factors,
        up_first_moment,
        up_second_moment,
    )
    return pl.pallas_call(
        deliver,
        out_shape=outs,
        in_specs=[any_space] * 7,
        out_specs=[hbm] * 7,
        scratch_shapes=[vm(out.shape, out.dtype) for out in outs] + [dma((14,))],
        compiler_params=pltpu.CompilerParams(vmem_limit_bytes=VMEM_BYTES),
        name="deliver",
    )(*results)


def solution(mesh):
    both = ("stripe", "tensor")
    return jax.shard_map(
        functools.partial(on_device, mesh.shape["stripe"], mesh.shape["dp"], mesh.shape["tensor"]),
        mesh=mesh,
        in_specs=(
            P("dp", both),
            P("dp", "tensor"),
            P("stripe", "tensor"),
            P("dp", None),
            P("dp", None),
            P("dp", None, both),
            P("dp", None, both),
            P("dp", None, both),
            P("dp", None, "tensor"),
            P("dp", None, "tensor"),
            P("dp", None, "tensor"),
        ),
        out_specs=(
            P("dp", both),
            P("dp", None, both),
            P("dp", None, both),
            P("dp", None, both),
            P("dp", None, "tensor"),
            P("dp", None, "tensor"),
            P("dp", None, "tensor"),
        ),
        check_vma=False,
    )
```

```python
import functools

import jax
import jax.numpy as jnp
from jax import lax
from jax.experimental import pallas as pl
from jax.experimental.pallas import tpu as pltpu
from jax.sharding import PartitionSpec as P

BLK = 128
RANK = 16
DOWN = 48
FAC = 64
PIECES = 4
SKEW = 2
AHEAD = 4
VMEM_BYTES = 62 * 1024 * 1024

adapter_scale = 2.0
beta_one = 0.9
beta_two = 0.95
adam_rate = 0.001
adam_eps = 1e-08
adam_steps = 10.0

F32 = jnp.float32
BF16 = jnp.bfloat16
MESH = pl.DeviceIdType.MESH

AT_GREET = 0
AT_EXCHANGE = 1
AT_RELAY = 3
AT_FORWARD = 5
AT_PROJECT = 8
AT_STRIPE_SUM = 10
AT_TENSOR_SUM = 12
AT_STRIPE_SPREAD = 15
AT_GRADIENT = 17
AT_ADAPTER = 18
AT_GROUP_SUM = 20
AT_OWN_SUM = 21
AT_RELAY_SUM = 22
AT_HALF_SUM = 25
AT_UP_ADAM = 27


def adam(params, moment, second, gradient):
    moment_new = beta_one * moment + (1.0 - beta_one) * gradient
    second_new = beta_two * second + (1.0 - beta_two) * (gradient * gradient)
    first_fix = moment_new / (1.0 - beta_one**adam_steps)
    second_fix = second_new / (1.0 - beta_two**adam_steps)
    stepped = params.astype(F32) - adam_rate * first_fix / (jnp.sqrt(second_fix) + adam_eps)
    return stepped.astype(BF16), moment_new, second_new


def kernel(
    S, NP, NT,
    ten_ref, fill_ref,
    x_in, a_in, w_in, dn_in, dm_in, dv_in, up_in, um_in, uv_in,
    out_o, dn_o, dm_o, dv_o, up_o, um_o, uv_o,
    av, wv, xv, fac, pv, rv,
    lp, xrs, xs, zrs, lb, fac_held, sum_held,
    gl, ul, gp, grs, go, gs, gz, ux, acc, ov,
    dmv, dvv, umv, uvv, upv, dnn, upn,
    load_sem, a_sem, w_sem, out_sem, store_sem,
    line_send, line_recv,
    fac_send, fac_recv,
    xr_send, xr_recv, zr_send, zr_recv, za_send, za_recv, xa_send, xa_recv,
    gr_send, gr_recv, gz_send, gz_recv, ux_send, ux_recv, hello,
    out_send, relay_send, relay_recv,
):
    G = NP // 2
    TOK, C = av.shape
    D = xv.shape[1]
    NB = TOK // BLK
    QT = TOK // S
    CQ = C // S
    HALF = CQ // 2
    PR = TOK // PIECES
    CHUNK = wv.shape[0] // NT
    s = lax.axis_index("stripe")
    p = lax.axis_index("dp")
    t = lax.axis_index("tensor")
    zh = lax.div(p, G)
    m = lax.rem(p, G)
    pz = (1 - zh) * G + m

    def remote(src, dst, send, recv, device):
        return pltpu.make_async_remote_copy(
            src_ref=src, dst_ref=dst, send_sem=send, recv_sem=recv, device_id=device, device_id_type=MESH
        )

    def other(axis, here, size, o):
        return {axis: lax.rem(here + o, size)}

    def group_peer(o):
        return zh * G + lax.rem(m + o, G)

    quarter = pl.ds(pl.multiple_of(s * CQ, CQ), CQ)
    my_tokens = pl.ds(pl.multiple_of(s * QT, QT), QT)
    loads = [
        pltpu.make_async_copy(dn_in.at[0], fac.at[p, pl.ds(0, DOWN)], load_sem.at[0]),
        pltpu.make_async_copy(up_in.at[0, :, quarter], fac.at[p, pl.ds(DOWN, RANK)], load_sem.at[1]),
        pltpu.make_async_copy(x_in, xv, load_sem.at[2]),
        pltpu.make_async_copy(dm_in.at[0], dmv, load_sem.at[3]),
        pltpu.make_async_copy(dv_in.at[0], dvv, load_sem.at[4]),
        pltpu.make_async_copy(um_in.at[0], umv, load_sem.at[5]),
        pltpu.make_async_copy(uv_in.at[0], uvv, load_sem.at[6]),
        pltpu.make_async_copy(up_in.at[0], upv, load_sem.at[7]),
    ]

    def order(i):
        inner = jnp.where(lax.rem(i, 2) == 0, NT - 1 - lax.div(i, 2), lax.div(i, 2))
        return jnp.where(t == 0, NT - 1 - i, jnp.where(t == NT - 1, i, inner))

    def w_load(j):
        rows = pl.ds(pl.multiple_of(j * CHUNK, CHUNK), CHUNK)
        return pltpu.make_async_copy(w_in.at[rows], wv.at[rows], w_sem.at[j])

    def a_load(q):
        rows = pl.ds(q * PR, PR)
        return pltpu.make_async_copy(a_in.at[rows], av.at[rows], a_sem.at[q])

    a_load(0).start()
    w_load(order(jnp.int32(0))).start()
    for load in loads[:2]:
        load.start()
    for q in range(1, PIECES):
        a_load(q).start()
    for i in range(1, NT):
        w_load(order(jnp.int32(i))).start()
    for load in loads[2:]:
        load.start()

    z = zh * NT + t
    after = {"dp": jnp.where(t == NT - 1, p + G, p), "tensor": lax.rem(t + 1, NT)}
    before = {"dp": jnp.where(t == 0, p - G, p), "tensor": lax.rem(t + NT - 1, NT)}
    has_after, has_before = z < 2 * NT - 1, z > 0
    barrier = pltpu.get_barrier_semaphore()
    partners = [other("stripe", s, S, o) for o in range(1, S)]
    partners += [{"dp": group_peer(o)} for o in range(1, G)]
    for partner in partners:
        pl.semaphore_signal(barrier, inc=1, device_id=partner, device_id_type=MESH)
    for there, partner in ((has_after, after), (has_before, before)):

        @pl.when(there)
        def _(partner=partner):
            pl.semaphore_signal(barrier, inc=1, device_id=partner, device_id_type=MESH)

    def multiply(i):
        j = order(i)
        w_load(j).wait()
        part = lax.dot_general(
            av[...],
            wv[pl.ds(pl.multiple_of(j * CHUNK, CHUNK), CHUNK), :],
            (((1,), (1,)), ((), ())),
            preferred_element_type=F32,
        )
        pv[j] = part.astype(BF16)

    def begin(q):
        a_load(q).wait()

        @pl.loop(q * PR // BLK, (q + 1) * PR // BLK)
        def _(b):
            rows = pl.ds(pl.multiple_of(b * BLK, BLK), BLK)
            place = lax.broadcasted_iota(jnp.int32, (BLK, C), 0)
            block = av[rows, :]
            av[rows, :] = jnp.where(place < fill_ref[0, b], block, jnp.zeros_like(block))

        j = order(jnp.int32(0))
        if q == 0:
            w_load(j).wait()
        rows = pl.ds(q * PR, PR)
        part = lax.dot_general(
            av[rows, :],
            wv[pl.ds(pl.multiple_of(j * CHUNK, CHUNK), CHUNK), :],
            (((1,), (1,)), ((), ())),
            preferred_element_type=F32,
        )
        pv[j, rows, :] = part.astype(BF16)

    begin(0)
    loads[0].wait()
    loads[1].wait()
    pl.semaphore_wait(barrier, len(partners) + jnp.where(has_after & has_before, 2, 1))

    def greet(slot):
        for way, to, there in ((0, after, has_after), (1, before, has_before)):
            r = z if way == 0 else 2 * NT - 1 - z
            if slot >= 1:

                @pl.when(r >= slot + 1)
                def _(way=way):
                    pl.semaphore_wait(hello.at[way, slot], 1)

            if slot + 1 < NT:

                @pl.when((r >= slot + 1) & there)
                def _(way=way, to=to):
                    pl.semaphore_signal(hello.at[way, slot + 1], inc=1, device_id=to, device_id_type=MESH)

    def rank(way):
        return t if way == 0 else NT - 1 - t

    def line_copy(way, u):
        k, q = lax.div(u, PIECES), lax.rem(u, PIECES)
        j = NT - 1 - k if way == 0 else k
        rows = pl.ds(pl.multiple_of(q * PR, PR), PR)
        to = t + 1 if way == 0 else t - 1
        return j, rows, remote(
            pv.at[j, rows], rv.at[way, j, rows], line_send.at[j, q], line_recv.at[way, j, q], {"tensor": to}
        )

    def line_step(v):
        for way in range(2):
            r = rank(way)
            u = v - SKEW * r

            @pl.when((u >= 0) & (u < (NT - 1 - r) * PIECES))
            def _(way=way, r=r, u=u):
                j, rows, copy = line_copy(way, u)

                @pl.when(r > 0)
                def _():
                    copy.wait_recv()
                    pv[j, rows, :] = (pv[j, rows, :].astype(F32) + rv[way, j, rows, :].astype(F32)).astype(BF16)

                @pl.when(u >= AHEAD)
                def _():
                    line_copy(way, u - AHEAD)[2].wait_send()

                copy.start()

    greet(0)
    line_step(jnp.int32(0))

    def fac_copy(slot, i, device):
        return remote(fac.at[slot], fac.at[slot], fac_send.at[i], fac_recv.at[slot], device)

    def xr_copy(o):
        to = lax.rem(s + o, S)
        lanes = pl.ds(pl.multiple_of(to * QT, QT), QT)
        return remote(lp.at[:, lanes], xrs.at[s], xr_send.at[o], xr_recv.at[s], {"stripe": to})

    def owner(g):
        return (g + 1) % NT

    def section(g):
        return pl.ds(g * RANK, RANK)

    def zr_copy(g):
        return remote(xs.at[section(g)], zrs.at[g, t], zr_send.at[g], zr_recv.at[g, t], {"tensor": owner(g)})

    def za_copy(g, o):
        part = lb.at[section(g), my_tokens]
        return remote(part, part, za_send.at[g, o], za_recv.at[g], other("tensor", t, NT, o))

    def xa_copy(o):
        part = lb.at[:, my_tokens]
        return remote(part, part, xa_send.at[o], xa_recv.at[s], other("stripe", s, S, o))

    def gr_copy(o, half):
        to = lax.rem(m + o, G)
        return remote(
            gp.at[to, half], grs.at[m, half], gr_send.at[o, half], gr_recv.at[m, half], {"dp": zh * G + to}
        )

    MID = NT // 2
    far = lax.rem(t + MID, NT)
    half_way = {"dp": jnp.where(t < MID, m, G + m), "tensor": far}
    is_relay = (z >= MID) & (z < NT + MID)

    def to_relay(src, buf, i):
        return remote(src, buf.at[zh], out_send.at[i], relay_recv.at[i, zh], half_way)

    def from_relay(buf, dst, i, side, recv):
        return remote(
            buf.at[side], dst, relay_send.at[i, side], recv, {"dp": (1 - side) * G + m, "tensor": far}
        )

    def fac_relay(side):
        slot = side * G + m
        return from_relay(fac_held, fac.at[slot], 0, side, fac_recv.at[slot])

    def gz_copy():
        return remote(gs, gz, gz_send, gz_recv, {"dp": pz})

    def ux_copy(o):
        return remote(ux.at[s], ux.at[s], ux_send.at[o], ux_recv.at[s], other("stripe", s, S, o))

    for o in range(1, G):
        fac_copy(p, o, {"dp": group_peer(o)}).start()

    for q in range(1, PIECES):
        begin(q)
    greet(1)

    def exchange():
        to_relay(fac.at[p], fac_held, 0).start()

    def relay():
        @pl.when(is_relay)
        def _():
            for side in range(2):
                remote(gs, fac_held.at[side], gz_send, relay_recv.at[0, side], {"dp": pz}).wait_recv()
                fac_relay(side).start()

    def forward():
        fac_copy(pz, 0, {"dp": pz}).wait_recv()
        for o in range(1, G):
            fac_copy(pz, G + o, {"dp": group_peer(o)}).start()

    def project():
        for o in range(1, G):
            fac_copy(zh * G + lax.rem(m + o, G), 0, {"dp": pz}).wait_recv()
            fac_copy((1 - zh) * G + lax.rem(m + o, G), 0, {"dp": pz}).wait_recv()
        loads[2].wait()
        last = s == S - 1
        zero = jnp.zeros((RANK, BLK), F32)

        @pl.loop(0, NB)
        def _(b):
            rows = pl.ds(pl.multiple_of(b * BLK, BLK), BLK)
            chosen = fac[ten_ref[0, b]]
            nt = (((1,), (1,)), ((), ()))
            low = lax.dot_general(chosen[:DOWN], xv[rows, :], nt, preferred_element_type=F32)
            grad = av[rows, quarter]
            first = lax.dot_general(chosen[DOWN:, :HALF], grad[:, :HALF], nt, preferred_element_type=F32)
            second = lax.dot_general(chosen[DOWN:, HALF:], grad[:, HALF:], nt, preferred_element_type=F32)
            both = jnp.concatenate(
                [
                    low,
                    jnp.where(last, zero, first + second),
                    jnp.where(last, first, zero),
                    jnp.where(last, second, zero),
                ],
                axis=0,
            )
            lp[:, rows] = (adapter_scale * both).astype(BF16)

        for o in range(1, S):
            xr_copy(o).start()

    def stripe_sum():
        total = lp[:, my_tokens].astype(F32)
        for o in range(1, S):
            src = lax.rem(s + o, S)
            remote(xs, xrs.at[src], xr_send.at[0], xr_recv.at[src], {"dp": pz}).wait_recv()
            total += xrs[src].astype(F32)
        xs[...] = total.astype(BF16)
        for g in range(6):

            @pl.when(t != owner(g))
            def _(g=g):
                zr_copy(g).start()

    def tensor_sum():
        for g in range(6):

            @pl.when(t == owner(g))
            def _(g=g):
                def add(o, total):
                    src = lax.rem(t + o, NT)
                    remote(
                        xs.at[section(g)], zrs.at[g, src], zr_send.at[g], zr_recv.at[g, src], {"dp": pz}
                    ).wait_recv()
                    return total + zrs[g, src].astype(F32)

                total = lax.fori_loop(1, NT, add, xs[section(g), :].astype(F32))
                lb[section(g), my_tokens] = total.astype(BF16)
                for o in range(1, NT):
                    za_copy(g, o).start()

    def stripe_spread():
        for g in range(6):

            @pl.when(t != owner(g))
            def _(g=g):
                za_copy(g, 1).wait_recv()

        for o in range(1, S):
            xa_copy(o).start()

    group = min(4, NP)

    def gradient():
        for o in range(1, S):
            src = lax.rem(s + o, S)
            part = lb.at[:, pl.ds(pl.multiple_of(src * QT, QT), QT)]
            remote(part, part, xa_send.at[0], xa_recv.at[src], {"dp": pz}).wait_recv()
        block_of = lax.div(lax.broadcasted_iota(jnp.int32, (1, TOK), 1), BLK)
        tenant = jnp.zeros((1, TOK), jnp.int32)
        for b in range(NB):
            tenant = jnp.where(block_of == b, ten_ref[0, b], tenant)
        last = s == S - 1
        sec_first = jnp.where(last, RANK, 0)
        sec_second = jnp.where(last, 2 * RANK, 0)

        @pl.loop(0, NP)
        def _(n):
            here = jnp.where(tenant == n, 1.0, 0.0).astype(BF16)
            gl[pl.ds(pl.multiple_of(n * DOWN, RANK), DOWN), :] = lb[pl.ds(DOWN, DOWN), :] * here
            rows = pl.ds(pl.multiple_of(n * RANK, RANK), RANK)
            ul[0, rows, :] = lb[pl.ds(pl.multiple_of(sec_first, RANK), RANK), :] * here
            ul[1, rows, :] = lb[pl.ds(pl.multiple_of(sec_second, RANK), RANK), :] * here

        @pl.loop(0, NP // group)
        def _(i):
            rows = pl.ds(pl.multiple_of(i * group * DOWN, RANK), group * DOWN)
            part = jnp.dot(gl[rows, :], xv[...], preferred_element_type=F32).astype(BF16)
            for e in range(group):
                n = i * group + e
                gp[lax.rem(n, G), lax.div(n, G), :DOWN, :] = part[e * DOWN : (e + 1) * DOWN]

        for h in range(2):
            lanes = pl.ds(pl.multiple_of(s * CQ + h * HALF, HALF), HALF)
            part = jnp.dot(ul[h], av[:, lanes], preferred_element_type=F32).astype(BF16)
            for n in range(NP):
                gp[n % G, n // G, DOWN:, h * HALF : (h + 1) * HALF] = part[n * RANK : (n + 1) * RANK]

        for half in (1 - zh, zh):
            for o in range(1, G):
                gr_copy(o, half).start()

    def adapter():
        @pl.loop(0, NB)
        def _(b):
            rows = pl.ds(pl.multiple_of(b * BLK, BLK), BLK)
            down = fac[ten_ref[0, b]][:DOWN]
            extra = lax.dot_general(
                lb[pl.ds(DOWN, DOWN), rows], down, (((0,), (0,)), ((), ())), preferred_element_type=F32
            )
            acc[rows, :] = extra + pv[t, rows, :].astype(F32)

    def total(half):
        value = gp[m, half].astype(F32)
        for o in range(1, G):
            src = lax.rem(m + o, G)
            remote(
                gp.at[0, half], grs.at[src, half], gr_send.at[0, half], gr_recv.at[src, half], {"dp": pz}
            ).wait_recv()
            value += grs[src, half].astype(F32)
        return value

    def group_sum():
        gs[...] = total(1 - zh).astype(BF16)
        gz_copy().start()

    def own_sum():
        go[...] = total(zh)

    def half_sum():
        gz_copy().wait_recv()
        grad = go[...] + gz[...].astype(F32)
        ux[s] = grad[DOWN:]
        for o in range(1, S):
            ux_copy(o).start()
        for load in loads[3:]:
            load.wait()
        dnn[...], dmv[...], dvv[...] = adam(fac[p, :DOWN, :], dmv[...], dvv[...], grad[:DOWN])
        for store in stores[:3]:
            store.start()

    def up_adam():
        for o in range(1, S):
            src = lax.rem(s + o, S)
            remote(ux.at[src], ux.at[src], ux_send.at[0], ux_recv.at[src], {"dp": pz}).wait_recv()
        for i in range(S):
            lanes = pl.ds(i * CQ, CQ)
            upn[:, lanes], umv[:, lanes], uvv[:, lanes] = adam(
                upv[:, lanes], umv[:, lanes], uvv[:, lanes], ux[i]
            )
        for store in stores[3:]:
            store.start()

    stores = [
        pltpu.make_async_copy(dnn, dn_o.at[0], store_sem.at[0]),
        pltpu.make_async_copy(dmv, dm_o.at[0], store_sem.at[1]),
        pltpu.make_async_copy(dvv, dv_o.at[0], store_sem.at[2]),
        pltpu.make_async_copy(upn, up_o.at[0], store_sem.at[3]),
        pltpu.make_async_copy(umv, um_o.at[0], store_sem.at[4]),
        pltpu.make_async_copy(uvv, uv_o.at[0], store_sem.at[5]),
    ]

    greetings = range(2, NT)
    stages = [(AT_GREET + max(1, slot - 2), functools.partial(greet, slot)) for slot in greetings]
    stages += [
        (AT_EXCHANGE, exchange),
        (AT_RELAY, relay),
        (AT_FORWARD, forward),
        (AT_PROJECT, project),
        (AT_STRIPE_SUM, stripe_sum),
        (AT_TENSOR_SUM, tensor_sum),
        (AT_STRIPE_SPREAD, stripe_spread),
        (AT_GRADIENT, gradient),
        (AT_ADAPTER, adapter),
        (AT_GROUP_SUM, group_sum),
        (AT_OWN_SUM, own_sum),
        (AT_HALF_SUM, half_sum),
        (AT_UP_ADAM, up_adam),
    ]
    steps = max((NT - 1 - r) * PIECES + SKEW * r for r in range(NT - 1))
    steps = max(steps, AT_UP_ADAM + 1, NT)

    @pl.loop(1, steps)
    def _(v):
        line_step(v)

        @pl.when(v < NT)
        def _():
            multiply(v)

        for at, stage in stages:
            pl.when(v == at)(stage)

    def finish(q):
        rows = pl.ds(q * PR, PR)
        for way in range(2):

            @pl.when(rank(way) > 0)
            def _(way=way):
                part = rv.at[way, t, rows]
                remote(part, part, line_send.at[t, q], line_recv.at[way, t, q], {"dp": pz}).wait_recv()
                acc[rows, :] += rv[way, t, rows, :].astype(F32)

        ov[rows, :] = acc[rows, :].astype(BF16)
        return pltpu.make_async_copy(ov.at[rows], out_o.at[rows], out_sem.at[q])

    writes = []
    for q in range(PIECES):
        write = finish(q)
        write.start()
        writes.append(write)

    for way in range(2):
        r = rank(way)

        @pl.when(r < NT - 1)
        def _(way=way, r=r):
            for back in range(AHEAD):
                line_copy(way, (NT - 1 - r) * PIECES - AHEAD + back)[2].wait_send()

    for o in range(1, G):
        fac_copy(p, o, {"dp": group_peer(o)}).wait_send()
        fac_copy(pz, G + o, {"dp": group_peer(o)}).wait_send()
        gr_copy(o, 0).wait_send()
        gr_copy(o, 1).wait_send()
    for o in range(1, S):
        xr_copy(o).wait_send()
        xa_copy(o).wait_send()
        ux_copy(o).wait_send()
    for g in range(6):

        @pl.when(t != owner(g))
        def _(g=g):
            zr_copy(g).wait_send()

        @pl.when(t == owner(g))
        def _(g=g):
            for o in range(1, NT):
                za_copy(g, o).wait_send()

    to_relay(fac.at[p], fac_held, 0).wait_send()
    gz_copy().wait_send()

    @pl.when(is_relay)
    def _():
        for side in range(2):
            fac_relay(side).wait_send()

    for store in stores:
        store.wait()
    for write in writes:
        write.wait()


def deliver(*refs):
    ins, outs, held, (sems,) = refs[:7], refs[7:14], refs[14:21], refs[21:]
    copies = [pltpu.make_async_copy(ins[i], held[i], sems.at[i]) for i in range(7)]
    for copy in copies:
        copy.start()
    writes = [pltpu.make_async_copy(held[i], outs[i], sems.at[7 + i]) for i in range(7)]
    for copy, write in zip(copies, writes):
        copy.wait()
        write.start()
    for write in writes:
        write.wait()


def on_device(
    S, NP, NT,
    normed_layer_input,
    projection_output_gradient,
    frozen_projection_weight,
    block_owner_tenant,
    block_token_fill,
    adapter_down_factors,
    down_first_moment,
    down_second_moment,
    adapter_up_factors,
    up_first_moment,
    up_second_moment,
):
    tok, d = normed_layer_input.shape
    c = projection_output_gradient.shape[1]
    w_rows = frozen_projection_weight.shape[0]
    G = NP // 2
    qt = tok // S
    any_space = pl.BlockSpec(memory_space=pl.ANY)
    hbm = pl.BlockSpec(memory_space=pltpu.HBM)
    smem = pl.BlockSpec(memory_space=pltpu.SMEM)
    outs = (
        jax.ShapeDtypeStruct((tok, d), BF16),
        jax.ShapeDtypeStruct(adapter_down_factors.shape, BF16),
        jax.ShapeDtypeStruct(down_first_moment.shape, F32),
        jax.ShapeDtypeStruct(down_second_moment.shape, F32),
        jax.ShapeDtypeStruct(adapter_up_factors.shape, BF16),
        jax.ShapeDtypeStruct(up_first_moment.shape, F32),
        jax.ShapeDtypeStruct(up_second_moment.shape, F32),
    )
    vm, dma = pltpu.VMEM, pltpu.SemaphoreType.DMA
    scratch = [
        vm((tok, c), BF16),
        vm((w_rows, c), BF16),
        vm((tok, d), BF16),
        vm((NP, FAC, d), BF16),
        vm((NT, tok, w_rows // NT), BF16),
        vm((2, NT, tok, w_rows // NT), BF16),
        vm((2 * DOWN, tok), BF16),
        vm((S, 2 * DOWN, qt), BF16),
        vm((2 * DOWN, qt), BF16),
        vm((6, NT, RANK, qt), BF16),
        vm((2 * DOWN, tok), BF16),
        vm((2, FAC, d), BF16),
        vm((2, FAC, d), BF16),
        vm((NP * DOWN, tok), BF16),
        vm((2, NP * RANK, tok), BF16),
        vm((G, 2, FAC, d), BF16),
        vm((G, 2, FAC, d), BF16),
        vm((FAC, d), F32),
        vm((FAC, d), BF16),
        vm((FAC, d), BF16),
        vm((S, RANK, c // S), F32),
        vm((tok, d), F32),
        vm((tok, d), BF16),
        vm((DOWN, d), F32),
        vm((DOWN, d), F32),
        vm((RANK, c), F32),
        vm((RANK, c), F32),
        vm((RANK, c), BF16),
        vm((DOWN, d), BF16),
        vm((RANK, c), BF16),
        dma((8,)), dma((PIECES,)), dma((NT,)), dma((PIECES,)), dma((6,)),
        dma((NT, PIECES)), dma((2, NT, PIECES)),
        dma((2 * G,)), dma((NP,)),
        dma((S,)), dma((S,)), dma((6,)), dma((6, NT)), dma((6, NT)), dma((6,)), dma((S,)), dma((S,)),
        dma((G, 2)), dma((G, 2)), dma, dma, dma((S,)), dma((S,)), pltpu.SemaphoreType.REGULAR((2, NT)),
        dma((2,)), dma((2, 2)), dma((2, 2)),
    ]
    results = pl.pallas_call(
        functools.partial(kernel, S, NP, NT),
        out_shape=outs,
        in_specs=[smem] * 2 + [hbm] * 9,
        out_specs=[any_space] * 7,
        scratch_shapes=scratch,
        compiler_params=pltpu.CompilerParams(
            collective_id=0, has_side_effects=True, vmem_limit_bytes=VMEM_BYTES
        ),
        cost_estimate=pl.CostEstimate(
            flops=2 * tok * c * w_rows, bytes_accessed=2 * (tok * c + w_rows * c), transcendentals=0
        ),
        name="united_backward",
    )(
        block_owner_tenant.T,
        block_token_fill.T,
        normed_layer_input,
        projection_output_gradient,
        frozen_projection_weight,
        adapter_down_factors,
        down_first_moment,
        down_second_moment,
        adapter_up_factors,
        up_first_moment,
        up_second_moment,
    )
    return pl.pallas_call(
        deliver,
        out_shape=outs,
        in_specs=[any_space] * 7,
        out_specs=[hbm] * 7,
        scratch_shapes=[vm(out.shape, out.dtype) for out in outs] + [dma((14,))],
        compiler_params=pltpu.CompilerParams(vmem_limit_bytes=VMEM_BYTES),
        name="deliver",
    )(*results)


def solution(mesh):
    both = ("stripe", "tensor")
    return jax.shard_map(
        functools.partial(on_device, mesh.shape["stripe"], mesh.shape["dp"], mesh.shape["tensor"]),
        mesh=mesh,
        in_specs=(
            P("dp", both),
            P("dp", "tensor"),
            P("stripe", "tensor"),
            P("dp", None),
            P("dp", None),
            P("dp", None, both),
            P("dp", None, both),
            P("dp", None, both),
            P("dp", None, "tensor"),
            P("dp", None, "tensor"),
            P("dp", None, "tensor"),
        ),
        out_specs=(
            P("dp", both),
            P("dp", None, both),
            P("dp", None, both),
            P("dp", None, both),
            P("dp", None, "tensor"),
            P("dp", None, "tensor"),
            P("dp", None, "tensor"),
        ),
        check_vma=False,
    )
```
